128 devices in a mesh: dp: 4 (over x), ctx: 32 (over z, y, core).
Axes of the slice: x: 4, y: 4, z: 4, core: 2. Of those that a mesh axis runs over, the one named last changes fastest.
Arguments:
- queries: bfloat16 [4, 4096, 2048], P('dp', 'ctx'), may hold values from -21 to 21
- key_rows: bfloat16 [4, 4096, 512], P('dp', 'ctx'), may hold values from -21 to 21
- value_row_blocks: bfloat16 [4, 4096, 512], P('dp', 'ctx'), may hold values from -6 to 6
- out_grad: bfloat16 [4, 4096, 2048], P('dp', 'ctx'), may hold values from -6 to 6
- segment_ids: int32 [4, 4096], P('dp', 'ctx'), may hold values from 0 to 15, never falling along the last dimension, each value on 1 to 2304 neighbouring positions
- block_plan: int32 [4, 32], P('dp', 'ctx'), may hold values from 0 to 3, as said below
Outputs:
- attended: bfloat16 [4, 4096, 2048], P('dp', 'ctx')
- query_grad: bfloat16 [4, 4096, 2048], P('dp', 'ctx')
- key_grad: bfloat16 [4, 4096, 512], P('dp', 'ctx')
- value_grad: bfloat16 [4, 4096, 512], P('dp', 'ctx')
The draws below stay inside these ranges and needn't reach their ends.
Inputs may be any that keep to these rules, and one draw needn't show every extreme that they name: For every block b, block_plan[d, b] over the 4 values of d names every sequence once.
All inputs are finite; a program needn't handle non-finite values.
Results may differ from the reference program's by a relative error of at most 0.025.
Values may be sent and summed in bfloat16 or wider, within the bound.
A program may use at most 128 MiB of HBM per device.

```python
import math
import jax
import jax.numpy as jnp
import numpy as np
from jax import lax

QUERY_HEADS = 16
KEY_VALUE_HEADS = 4
HEAD_SIZE = 128
BLK = 128
SEQUENCE_COUNT = 4
SEQUENCE_LENGTH = 4096
NBLK = 32
DOCS = 16
SEG_MOST = 2304


def draw_queries(key, part):
    query_group_width = QUERY_HEADS // KEY_VALUE_HEADS
    complete_shape = (SEQUENCE_COUNT, SEQUENCE_LENGTH, KEY_VALUE_HEADS, query_group_width, HEAD_SIZE)
    base_offset = jnp.clip(jax.random.normal(jax.random.fold_in(key, 1), complete_shape, jnp.float32), -6.0, 6.0)
    return base_offset.reshape(SEQUENCE_COUNT, SEQUENCE_LENGTH, QUERY_HEADS * HEAD_SIZE).astype(jnp.bfloat16)


def draw_key_rows(key, part):
    complete_shape = (SEQUENCE_COUNT, SEQUENCE_LENGTH, KEY_VALUE_HEADS, HEAD_SIZE)
    base_offset = jnp.clip(jax.random.normal(jax.random.fold_in(key, 2), complete_shape, jnp.float32), -6.0, 6.0)
    return base_offset.reshape(SEQUENCE_COUNT, SEQUENCE_LENGTH, KEY_VALUE_HEADS * HEAD_SIZE).astype(jnp.bfloat16)


def draw_block_plan(key, part):
    block_keys = jax.random.split(key, NBLK)
    orders = jax.vmap(lambda one_key: jax.random.permutation(one_key, SEQUENCE_COUNT))(block_keys)
    return orders.T.astype(jnp.int32)


def block_levels(rng, shape, cuts, low, top_value):
    loudness, own = 1.0, jax.random.fold_in(rng, 6)
    for position, blocks in cuts:
        draws = jnp.exp(jax.random.uniform(jax.random.fold_in(own, position), (blocks,), jnp.float32, low / len(cuts), top_value / len(cuts)))
        loudness = loudness * jnp.repeat(draws, shape[position] // blocks).reshape([-1 if axis == position else 1 for axis in range(len(shape))])
    return loudness


def profile(count, total, most, slope):
    weights = [(1 << 20) // math.isqrt(grade ** slope) + 1 for grade in range(2, count + 1)]
    rest, holding = total - most - (count - 1), [1] * (count - 1)
    while rest > 0:
        free = [i for i in range(count - 1) if holding[i] < most]
        mass, left = sum([weights[i] for i in free]), rest
        for i in free:
            extra = min(most - holding[i], max(1, left * weights[i] // mass), rest)
            holding[i] = holding[i] + extra
            rest = rest - extra
    return np.array([most] + holding)


def uneven_parts(stream_key, amount, total, most, lean):
    if amount == 2:
        one = jax.random.randint(stream_key, (), max(1, total - most), min(most, total - 1) + 1)
        return jnp.stack([one, total - one])
    lengths = jnp.asarray(profile(amount, total, most, lean), jnp.int32)
    pairs = (amount - 1) // 2
    source_of, receiver = lengths[1:1 + 2 * pairs:2], lengths[2:2 + 2 * pairs:2]
    room = jnp.minimum(source_of - 1, most - receiver)
    shifted = jax.random.randint(jax.random.fold_in(stream_key, 1), (pairs,), 0, 1 << 20) % (room + 1)
    lengths = lengths.at[1:1 + 2 * pairs:2].set(source_of - shifted).at[2:2 + 2 * pairs:2].set(receiver + shifted)
    return lengths[jax.random.permutation(jax.random.fold_in(stream_key, 2), amount)]


def noise(key, dims, scale, limit, cuts=(), held_as=jnp.bfloat16):
    factor_of = block_levels(key, dims, cuts, -0.22, 0.18) if cuts else 1.0
    drawn = jax.random.normal(key, dims, jnp.float32) * scale * factor_of
    return jnp.minimum(jnp.maximum(drawn, -limit), limit).astype(held_as)


def setup_inputs(seed: int = 0) -> dict:
    splits = jax.random.split(jax.random.key(seed), 7)
    return {
        "queries": draw_queries(jax.random.fold_in(splits[6], 71), 0),
        "key_rows": draw_key_rows(jax.random.fold_in(splits[6], 71), 0),
        "value_row_blocks": noise(splits[2], (SEQUENCE_COUNT, SEQUENCE_LENGTH, KEY_VALUE_HEADS * HEAD_SIZE), 1.0, 6.0, ((0, 4), (1, 32))),
        "out_grad": noise(splits[3], (SEQUENCE_COUNT, SEQUENCE_LENGTH, QUERY_HEADS * HEAD_SIZE), 1.0, 6.0, ((0, 4), (1, 32))),
        "segment_ids": jax.vmap(lambda own: jnp.searchsorted(jnp.cumsum(uneven_parts(own, DOCS, SEQUENCE_LENGTH, SEG_MOST, 1)), jnp.arange(SEQUENCE_LENGTH), side="right"))(jax.random.split(splits[4], SEQUENCE_COUNT)).reshape((SEQUENCE_COUNT, SEQUENCE_LENGTH)).astype(jnp.int32),
        "block_plan": draw_block_plan(jax.random.fold_in(splits[6], 71), 0),
    }


def one_sequence(inputs):
    query_sequence, key_sequence, value_sequence, grad_sequence, segments_here = inputs
    query_group_width = QUERY_HEADS // KEY_VALUE_HEADS
    attn_scale = 1.0 / math.sqrt(HEAD_SIZE)
    qblock = min(512, SEQUENCE_LENGTH)
    block_total = SEQUENCE_LENGTH // qblock
    query_gathered = query_sequence.reshape(SEQUENCE_LENGTH, KEY_VALUE_HEADS, query_group_width, HEAD_SIZE).astype(jnp.float32)
    gradient_gathered = grad_sequence.reshape(SEQUENCE_LENGTH, KEY_VALUE_HEADS, query_group_width, HEAD_SIZE).astype(jnp.float32)
    key_gathered = key_sequence.reshape(SEQUENCE_LENGTH, KEY_VALUE_HEADS, HEAD_SIZE).astype(jnp.float32)
    value_gathered = value_sequence.reshape(SEQUENCE_LENGTH, KEY_VALUE_HEADS, HEAD_SIZE).astype(jnp.float32)
    positions = jnp.arange(SEQUENCE_LENGTH, dtype=jnp.int32)

    def block_scores(block_index):
        first_row = (block_index * qblock).astype(jnp.int32)
        query_part = lax.dynamic_slice_in_dim(query_gathered, first_row, qblock, 0)
        segs_part = lax.dynamic_slice_in_dim(segments_here, first_row, qblock, 0)
        pos_part = first_row + jnp.arange(qblock, dtype=jnp.int32)
        visible = (segments_here[None, :] == segs_part[:, None]) & (positions[None, :] <= pos_part[:, None])
        scores = jnp.einsum('tkgd,skd->kgts', query_part, key_gathered) * attn_scale
        return (jnp.where(visible[None, None], scores, -jnp.inf), query_part, first_row)

    def forward_block(block_index):
        masked, _, _ = block_scores(block_index)
        row_max = lax.optimization_barrier(jnp.max(masked, axis=-1))
        log_total = row_max + jnp.log(lax.optimization_barrier(jnp.sum(jnp.exp(masked - row_max[..., None]), axis=-1)))
        weights = jnp.exp(masked - log_total[..., None])
        weight_half = lax.optimization_barrier(weights.astype(jnp.bfloat16)).astype(jnp.float32)
        attended = jnp.einsum('kgts,skd->tkgd', weight_half, value_gathered).astype(jnp.bfloat16)
        return (attended, log_total)
    block_ids = jnp.arange(block_total, dtype=jnp.int32)
    attended_blocks, log_totals = lax.map(forward_block, block_ids)

    def backward_block(carried, inputs_here):
        key_accumulator, value_accumulator = carried
        block_index, attended_part, log_total = inputs_here
        masked, query_part, first_row = block_scores(block_index)
        grad_part = lax.dynamic_slice_in_dim(gradient_gathered, first_row, qblock, 0)
        weights = jnp.exp(masked - log_total[..., None])
        weight_half = lax.optimization_barrier(weights.astype(jnp.bfloat16)).astype(jnp.float32)
        row_delta = lax.optimization_barrier(jnp.sum(grad_part * attended_part.astype(jnp.float32), axis=-1)).transpose(1, 2, 0)
        weight_grad = jnp.einsum('tkgd,skd->kgts', grad_part, value_gathered)
        score_grad = (weights * (weight_grad - row_delta[..., None]) * attn_scale).astype(jnp.bfloat16)
        score_grad = lax.optimization_barrier(score_grad).astype(jnp.float32)
        query_term = jnp.einsum('kgts,skd->tkgd', score_grad, key_gathered).astype(jnp.bfloat16)
        key_accumulator = key_accumulator + jnp.einsum('kgts,tkgd->skd', score_grad, query_part)
        value_accumulator = value_accumulator + jnp.einsum('kgts,tkgd->skd', weight_half, grad_part)
        return ((key_accumulator, value_accumulator), query_term)
    empty_block = jnp.zeros((SEQUENCE_LENGTH, KEY_VALUE_HEADS, HEAD_SIZE), jnp.float32)
    (key_accumulator, value_accumulator), query_terms = lax.scan(backward_block, (empty_block, empty_block), (block_ids, attended_blocks, log_totals))
    attended_seq = attended_blocks.reshape(SEQUENCE_LENGTH, QUERY_HEADS * HEAD_SIZE)
    dq_seq = query_terms.reshape(SEQUENCE_LENGTH, QUERY_HEADS * HEAD_SIZE)
    key_grad_sequence = key_accumulator.astype(jnp.bfloat16).reshape(SEQUENCE_LENGTH, KEY_VALUE_HEADS * HEAD_SIZE)
    value_grad_sequence = value_accumulator.astype(jnp.bfloat16).reshape(SEQUENCE_LENGTH, KEY_VALUE_HEADS * HEAD_SIZE)
    return (attended_seq, dq_seq, key_grad_sequence, value_grad_sequence)

def reference(queries, key_rows, value_row_blocks, out_grad, segment_ids, block_plan):
    block_count = SEQUENCE_LENGTH // BLK
    block_ids = jnp.arange(block_count, dtype=jnp.int32)
    seq_ids = jnp.arange(SEQUENCE_COUNT, dtype=jnp.int32)
    owners = block_plan[None, :, :] == seq_ids[:, None, None]
    source = lax.optimization_barrier(jnp.sum(jnp.where(owners, seq_ids[None, :, None], 0), axis=1)).astype(jnp.int32)

    def to_seq(whole_rows):
        shaped = whole_rows.reshape(SEQUENCE_COUNT, block_count, BLK, -1)
        return shaped[source, block_ids[None, :]].reshape(SEQUENCE_COUNT, SEQUENCE_LENGTH, -1)

    def to_plan(whole_rows):
        shaped = whole_rows.reshape(SEQUENCE_COUNT, block_count, BLK, -1)
        return shaped[block_plan, block_ids[None, :]].reshape(SEQUENCE_COUNT, SEQUENCE_LENGTH, -1)
    results = lax.map(one_sequence, (to_seq(queries), to_seq(key_rows), to_seq(value_row_blocks), to_seq(out_grad), segment_ids))
    return (to_plan(results[0]), to_plan(results[1]), to_plan(results[2]), to_plan(results[3]))
```

```python
import math

import jax
import jax.numpy as jnp
from jax import lax
from jax.experimental import pallas as pl
from jax.experimental.pallas import tpu as pltpu
from jax.sharding import PartitionSpec as P

MESH = pl.DeviceIdType.MESH
BF16 = jnp.bfloat16
F32 = jnp.float32

BLK = 128
HEAD = 128
GROUP = 4
GW = GROUP * HEAD
SIDE = 4
RING = 8
NBLK = 32
DOCS = 16
OFFSETS = (1, 3, 2)
CHUNK = 256
MOST = 10
PARTS = 2
PART = BLK // PARTS
NEG = -1e30


def place():
    x = lax.axis_index("dp")
    c = lax.axis_index("ctx")
    return x, lax.div(c, 8), lax.rem(lax.div(c, 2), 4), lax.rem(c, 2)


def remote(src, dst, send, recv, device):
    return pltpu.make_async_remote_copy(
        src_ref=src, dst_ref=dst, send_sem=send, recv_sem=recv, device_id=device, device_id_type=MESH
    )


def ahead(i, o):
    return lax.rem(i + o, 4)


def behind(i, o):
    return lax.rem(i + 4 - o, 4)


def ctx_of(z, y, core):
    return z * 8 + y * 2 + core


def lanes(i, width):
    return pl.ds(pl.multiple_of(i * width, width), width)


def one_hot(values, wanted):
    return jnp.where(values == wanted, 1.0, 0.0).astype(BF16)


def pick(weights, parts):
    width = parts[0].shape[1]
    tiles = []
    for t in range(width // 128):
        total = None
        for w, part in zip(weights, parts):
            term = part[:, t * 128 : (t + 1) * 128] * w
            total = term if total is None else total + term
        tiles.append(total)
    return tiles


def put(ref, tiles, base=None):
    for t, tile in enumerate(tiles):
        if base is None:
            ref[:, t * 128 : (t + 1) * 128] = tile
        else:
            ref[:, pl.ds(pl.multiple_of(base + t * 128, 128), 128)] = tile


def enter(devices):
    barrier = pltpu.get_barrier_semaphore()
    for device in devices:
        pl.semaphore_signal(barrier, inc=1, device_id=device, device_id_type=MESH)
    pl.semaphore_wait(barrier, len(devices))


def gather_kernel(
    q, k, v, g, seg, plan,
    qb, gb, kv, segs, planes,
    meta, a_kv, a_q, a_g, s_kv, s_q, s_g,
    xs, xr, zs, zr, ys, yr, cs, cr, fs, fr, ms, mr,
):
    x, z, y, core = place()
    ring = y * 2 + core
    x_dev = [(ahead(x, o), ctx_of(z, y, core)) for o in OFFSETS]
    z_dev = [(x, ctx_of(ahead(z, o), y, core)) for o in OFFSETS]
    y_dev = [(x, ctx_of(z, ahead(y, o), core)) for o in OFFSETS]
    w_dev = [(x, ctx_of(z, ahead(y, o), 1 - core)) for o in OFFSETS]
    c_dev = (x, ctx_of(z, y, 1 - core))

    meta[...] = jnp.broadcast_to(plan[...], (8, 128))
    meta[0:1, :] = seg[...]
    enter(x_dev + z_dev + y_dev + w_dev + [c_dev])

    x_cps = []
    for item in range(3 + 2 * PARTS):
        row = []
        for i, o in enumerate(OFFSETS):
            t = ahead(x, o)
            if item == 0:
                src, dst = meta, planes.at[x]
            elif item == 1:
                src, dst = k.at[:, lanes(t, HEAD)], a_kv.at[x, :, pl.ds(0, HEAD)]
            elif item == 2:
                src, dst = v.at[:, lanes(t, HEAD)], a_kv.at[x, :, pl.ds(HEAD, HEAD)]
            else:
                whole, land = ((q, a_q), (g, a_g))[(item - 3) // PARTS]
                rows = pl.ds(((item - 3) % PARTS) * PART, PART)
                src, dst = whole.at[rows, lanes(t, GW)], land.at[x, rows]
            cp = remote(src, dst, xs.at[i, item], xr.at[i, item], x_dev[i])
            cp.start()
            row.append(cp)
        x_cps.append(row)
    planes[x] = meta[...]
    a_kv[x, :, 0:HEAD] = k[:, lanes(x, HEAD)]
    a_kv[x, :, HEAD : 2 * HEAD] = v[:, lanes(x, HEAD)]
    a_q[x] = q[:, lanes(x, GW)]
    a_g[x] = g[:, lanes(x, GW)]

    def arrived(item):
        for cp in x_cps[item]:
            cp.wait_recv()

    arrived(0)
    m_z = []
    for i, o in enumerate(OFFSETS):
        cp = remote(planes.at[ahead(z, o)], segs.at[z, ring], zs.at[i, 0], zr.at[i, 0], z_dev[i])
        cp.start()
        m_z.append(cp)
    segs[z, ring] = planes[z]
    held = [planes[d, 1:2, :] for d in range(SIDE)]
    hots = [[one_hot(h, ahead(z, o)) for h in held] for o in OFFSETS]
    own_hot = [one_hot(h, z) for h in held]

    arrived(1)
    arrived(2)
    kv_z = []
    parts = [a_kv[d] for d in range(SIDE)]
    for i, o in enumerate(OFFSETS):
        put(s_kv.at[i], pick(hots[i], parts))
        cp = remote(s_kv.at[i], kv.at[z, ring], zs.at[i, 1], zr.at[i, 1], z_dev[i])
        cp.start()
        kv_z.append(cp)
    put(kv.at[z, ring], pick(own_hot, parts))

    y_cps, c_cps, f_cps = [], [], []

    def spread(p):
        zp = z if p == 0 else behind(z, OFFSETS[p - 1])
        row = []
        for i in range(3):
            cp = remote(kv.at[zp, ring], kv.at[zp, ring], ys.at[p, i], yr.at[p, i], y_dev[i])
            cp.start()
            row.append(cp)
        y_cps.append(row)
        cp = remote(kv.at[zp, ring], kv.at[zp, ring], cs.at[p], cr.at[p], c_dev)
        cp.start()
        c_cps.append(cp)

    def pass_on(p):
        zp = z if p == 0 else behind(z, OFFSETS[p - 1])
        for i, o in enumerate(OFFSETS):
            there = behind(y, o) * 2 + core
            y_cps[p][i].wait_recv()
            cp = remote(kv.at[zp, there], kv.at[zp, there], fs.at[p, i], fr.at[p, i], c_dev)
            cp.start()
            f_cps.append(cp)

    big_z = []

    def rows_over_z(item):
        which, part = (item - 3) // PARTS, (item - 3) % PARTS
        land, stage, out = ((a_q, s_q, qb), (a_g, s_g, gb))[which]
        rows = pl.ds(part * PART, PART)
        arrived(item)
        got = [land[d, part * PART : (part + 1) * PART] for d in range(SIDE)]
        for i, o in enumerate(OFFSETS):
            put(stage.at[i, rows], pick(hots[i], got))
            cp = remote(stage.at[i, rows], out.at[z, rows], zs.at[i, item - 1], zr.at[i, item - 1], z_dev[i])
            cp.start()
            big_z.append(cp)
        put(out.at[z, rows], pick(own_hot, got))

    spread(0)
    for p in range(3):
        kv_z[p].wait_recv()
        spread(p + 1)
    for cp in m_z:
        cp.wait_recv()
    s_cps = []
    for i, device in enumerate(y_dev + w_dev + [c_dev]):
        cp = remote(segs.at[:, ring], segs.at[:, ring], ms.at[i], mr.at[i], device)
        cp.start()
        s_cps.append(cp)
    items = list(range(3, 3 + 2 * PARTS))
    for p, item in enumerate(items):
        rows_over_z(item)
        if p < 4:
            pass_on(p)
    for p in range(len(items), 4):
        pass_on(p)

    for cp in big_z + c_cps + f_cps + s_cps:
        cp.wait()
    for row in x_cps:
        for cp in row:
            cp.wait_send()
    for cp in m_z + kv_z:
        cp.wait_send()
    for row in y_cps:
        for cp in row:
            cp.wait_send()


def nt(a, b):
    return lax.dot_general(a, b, (((1,), (1,)), ((), ())), preferred_element_type=F32)


def tn(a, b):
    return lax.dot_general(a, b, (((0,), (0,)), ((), ())), preferred_element_type=F32)


def nn(a, b):
    return lax.dot_general(a, b, (((1,), (0,)), ((), ())), preferred_element_type=F32)


def attend_kernel(q, g, kv, segs, att, dq, dkv, qs, gs, scores, acc, total):
    step = pl.program_id(0)
    ring = lax.rem(lax.axis_index("ctx"), 8)
    block = step * RING + ring
    scale = 1.0 / math.sqrt(HEAD)
    log2e = scale / math.log(2.0)

    @pl.when(step == 0)
    def _():
        total[...] = jnp.zeros_like(total)

    for h in range(GROUP):
        qs[h * BLK : (h + 1) * BLK, :] = q[0, :, h * HEAD : (h + 1) * HEAD]
        gs[h * BLK : (h + 1) * BLK, :] = g[0, :, h * HEAD : (h + 1) * HEAD]

    ids = segs[:, 0, :]
    counts = jnp.concatenate(
        [jnp.sum(jnp.where(ids < t, 1.0, 0.0), axis=0, keepdims=True) for t in range(DOCS)], axis=0
    )
    starts = jnp.sum(counts, axis=1, keepdims=True)
    mine = segs[block, 0:1, :]
    doc = lax.broadcasted_iota(jnp.int32, (DOCS, BLK), 0)
    first = jnp.sum(jnp.where(doc == mine, starts, 0.0), axis=0, keepdims=True)
    lowest = jnp.min(first).astype(jnp.int32)
    first = first.astype(jnp.int32)
    here = block * BLK + lax.broadcasted_iota(jnp.int32, (1, BLK), 1)
    begin = lax.div(lowest, CHUNK)
    end = lax.div(block, CHUNK // BLK) + 1

    def keys_of(j):
        return pl.ds(pl.multiple_of(j * CHUNK, CHUNK), CHUNK)

    def score_step(j, top):
        s = nt(kv[keys_of(j), 0:HEAD], qs[...])
        pos = j * CHUNK + lax.broadcasted_iota(jnp.int32, (CHUNK, BLK), 0)
        seen = (pos >= first) & (pos <= here)
        tops = []
        for h in range(GROUP):
            sl = slice(h * BLK, (h + 1) * BLK)
            sh = jnp.where(seen, s[:, sl], NEG)
            scores[j - begin, :, sl] = sh
            tops.append(jnp.max(sh, axis=0, keepdims=True))
        return jnp.maximum(top, jnp.concatenate(tops, axis=1))

    top = lax.fori_loop(begin, end, score_step, jnp.full((1, GW), NEG, F32))
    acc[...] = jnp.zeros_like(acc)

    def out_step(j, norm):
        p = jnp.exp2((scores[j - begin] - top) * log2e)
        scores[j - begin] = p
        acc[...] += tn(kv[keys_of(j), HEAD : 2 * HEAD], p.astype(BF16))
        return norm + jnp.sum(p, axis=0, keepdims=True)

    norm = lax.fori_loop(begin, end, out_step, jnp.zeros((1, GW), F32))
    inv = 1.0 / norm
    deltas = []
    for h in range(GROUP):
        sl = slice(h * BLK, (h + 1) * BLK)
        o = jnp.transpose(acc[:, sl] * inv[:, sl]).astype(BF16)
        att[0, :, sl] = o
        prod = gs[sl, :].astype(F32) * o.astype(F32)
        deltas.append(jnp.sum(jnp.transpose(prod), axis=0, keepdims=True))
    delta = jnp.concatenate(deltas, axis=1)
    acc[...] = jnp.zeros_like(acc)

    def grad_step(j, carry):
        rows = keys_of(j)
        w = scores[j - begin] * inv
        dp = nt(kv[rows, HEAD : 2 * HEAD], gs[...])
        ds = (w * (dp - delta)).astype(BF16)
        acc[...] += tn(kv[rows, 0:HEAD], ds)
        total[rows, 0:HEAD] += nn(ds, qs[...])
        total[rows, HEAD : 2 * HEAD] += nn(w.astype(BF16), gs[...])
        return carry

    lax.fori_loop(begin, end, grad_step, 0)
    for h in range(GROUP):
        sl = slice(h * BLK, (h + 1) * BLK)
        dq[0, :, sl] = jnp.transpose(acc[:, sl] * scale).astype(BF16)

    @pl.when(step == SIDE - 1)
    def _():
        dkv[:, 0:HEAD] = (total[:, 0:HEAD] * scale).astype(BF16)
        dkv[:, HEAD : 2 * HEAD] = total[:, HEAD : 2 * HEAD].astype(BF16)


def return_kernel(
    att, dq, dkv, planes,
    o_att, o_dq, o_k, o_v,
    r_a, r_d, r_kv, c_in, tot, y_in, fin, s_a, s_d, s_kv,
    xs, xr, zs, zr, ys, yr, cs, cr,
):
    x, z, y, core = place()
    x_dev = [(ahead(x, o), ctx_of(z, y, core)) for o in OFFSETS]
    z_dev = [(x, ctx_of(ahead(z, o), y, core)) for o in OFFSETS]
    y_dev = [(x, ctx_of(z, ahead(y, o), core)) for o in OFFSETS]
    c_dev = (x, ctx_of(z, y, 1 - core))
    enter(x_dev + z_dev + y_dev + [c_dev])

    owners = [ahead(y, o) for o in OFFSETS] + [y]
    c_cps = []
    for i, owner in enumerate(owners):
        cp = remote(dkv.at[:, owner, 1 - core], c_in.at[i], cs.at[i], cr.at[i], c_dev)
        cp.start()
        c_cps.append(cp)
    z_cps = []
    for item in range(2 * PARTS):
        src, land = ((att, r_a), (dq, r_d))[item // PARTS]
        rows = pl.ds((item % PARTS) * PART, PART)
        row = []
        for i, o in enumerate(OFFSETS):
            cp = remote(src.at[ahead(z, o), rows], land.at[z, rows], zs.at[i, item], zr.at[i, item], z_dev[i])
            cp.start()
            row.append(cp)
        z_cps.append(row)
    r_a[z] = att[z]
    r_d[z] = dq[z]
    y_cps = []
    for i, owner in enumerate(owners):
        c_cps[i].wait_recv()
        for b in range(SIDE):
            tot[i, b] = (dkv[b, owner, core].astype(F32) + c_in[i, b].astype(F32)).astype(BF16)
        if i < 3:
            cp = remote(tot.at[i], y_in.at[i], ys.at[i], yr.at[i], y_dev[i])
            cp.start()
            y_cps.append(cp)

    x_cps = []
    hots = [[one_hot(planes[ahead(x, o), 1:2, :], s) for s in range(SIDE)] for o in OFFSETS]
    own_hot = [one_hot(planes[x, 1:2, :], s) for s in range(SIDE)]

    def rows_over_x(item):
        which, part = item // PARTS, item % PARTS
        land, stage, out = ((r_a, s_a, o_att), (r_d, s_d, o_dq))[which]
        rows = pl.ds(part * PART, PART)
        for cp in z_cps[item]:
            cp.wait_recv()
        got = [land[s, part * PART : (part + 1) * PART] for s in range(SIDE)]
        for i in range(3):
            put(stage.at[i, rows], pick(hots[i], got))
            cp = remote(
                stage.at[i, rows], out.at[rows, lanes(x, GW)], xs.at[i, item], xr.at[i, item], x_dev[i]
            )
            cp.start()
            x_cps.append(cp)
        put(out.at[rows], pick(own_hot, got), x * GW)

    for item in range(2 * PARTS - 1):
        rows_over_x(item)

    for cp in y_cps:
        cp.wait_recv()
    f_cps = []
    for i, o in enumerate(OFFSETS):
        b = ahead(z, o)
        total = tot[3, b].astype(F32)
        for n in range(3):
            total = total + y_in[n, b].astype(F32)
        fin[i] = total.astype(BF16)
        cp = remote(fin.at[i], r_kv.at[z], zs.at[i, 2 * PARTS], zr.at[i, 2 * PARTS], z_dev[i])
        cp.start()
        f_cps.append(cp)
    total = tot[3, z].astype(F32)
    for n in range(3):
        total = total + y_in[n, z].astype(F32)
    r_kv[z] = total.astype(BF16)

    rows_over_x(2 * PARTS - 1)
    for cp in f_cps:
        cp.wait_recv()
    got = [r_kv[s] for s in range(SIDE)]
    for i in range(3):
        put(s_kv.at[i], pick(hots[i], got))
        for n, out in enumerate((o_k, o_v)):
            item = 2 * PARTS + n
            cp = remote(
                s_kv.at[i, :, pl.ds(n * HEAD, HEAD)], out.at[:, lanes(x, HEAD)],
                xs.at[i, item], xr.at[i, item], x_dev[i],
            )
            cp.start()
            x_cps.append(cp)
    mine = pick(own_hot, got)
    o_k[:, lanes(x, HEAD)] = mine[0]
    o_v[:, lanes(x, HEAD)] = mine[1]

    for cp in x_cps:
        cp.wait()
    for cp in c_cps + y_cps + f_cps:
        cp.wait_send()
    for row in z_cps:
        for cp in row:
            cp.wait_send()


def body(queries, key_rows, value_rows, out_grad, segment_ids, block_plan):
    vmem = pl.BlockSpec(memory_space=pltpu.VMEM)
    dma = pltpu.SemaphoreType.DMA
    shape = jax.ShapeDtypeStruct
    qb, gb, kv, segs, planes = pl.pallas_call(
        gather_kernel,
        out_shape=(
            shape((SIDE, BLK, GW), BF16),
            shape((SIDE, BLK, GW), BF16),
            shape((SIDE, RING, BLK, 2 * HEAD), BF16),
            shape((SIDE, RING, 8, 128), jnp.int32),
            shape((SIDE, 8, 128), jnp.int32),
        ),
        in_specs=[vmem] * 6,
        out_specs=(vmem,) * 5,
        scratch_shapes=[
            pltpu.VMEM((8, 128), jnp.int32),
            pltpu.VMEM((SIDE, BLK, 2 * HEAD), BF16),
            pltpu.VMEM((SIDE, BLK, GW), BF16),
            pltpu.VMEM((SIDE, BLK, GW), BF16),
            pltpu.VMEM((3, BLK, 2 * HEAD), BF16),
            pltpu.VMEM((3, BLK, GW), BF16),
            pltpu.VMEM((3, BLK, GW), BF16),
            dma((3, 3 + 2 * PARTS)),
            dma((3, 3 + 2 * PARTS)),
            dma((3, 2 + 2 * PARTS)),
            dma((3, 2 + 2 * PARTS)),
            dma((4, 3)),
            dma((4, 3)),
            dma((4,)),
            dma((4,)),
            dma((4, 3)),
            dma((4, 3)),
            dma((7,)),
            dma((7,)),
        ],
        compiler_params=pltpu.CompilerParams(
            collective_id=0, has_side_effects=True, vmem_limit_bytes=40 << 20
        ),
        name="gather_rows",
    )(queries[0], key_rows[0], value_rows[0], out_grad[0], segment_ids, block_plan)

    rows = pl.BlockSpec((1, BLK, GW), lambda i: (i, 0, 0))
    length = NBLK * BLK
    att, dq, dkv = pl.pallas_call(
        attend_kernel,
        grid=(SIDE,),
        out_shape=(
            shape((SIDE, BLK, GW), BF16),
            shape((SIDE, BLK, GW), BF16),
            shape((length, 2 * HEAD), BF16),
        ),
        in_specs=[
            rows,
            rows,
            pl.BlockSpec((length, 2 * HEAD), lambda i: (0, 0)),
            pl.BlockSpec((NBLK, 8, 128), lambda i: (0, 0, 0)),
        ],
        out_specs=(rows, rows, pl.BlockSpec((length, 2 * HEAD), lambda i: (0, 0))),
        scratch_shapes=[
            pltpu.VMEM((GROUP * BLK, HEAD), BF16),
            pltpu.VMEM((GROUP * BLK, HEAD), BF16),
            pltpu.VMEM((MOST, CHUNK, GW), F32),
            pltpu.VMEM((HEAD, GW), F32),
            pltpu.VMEM((length, 2 * HEAD), F32),
        ],
        compiler_params=pltpu.CompilerParams(vmem_limit_bytes=48 << 20),
        name="attend",
    )(qb, gb, kv.reshape(length, 2 * HEAD), segs.reshape(NBLK, 8, 128))

    o_att, o_dq, o_k, o_v = pl.pallas_call(
        return_kernel,
        out_shape=(
            shape((BLK, SIDE * GW), BF16),
            shape((BLK, SIDE * GW), BF16),
            shape((BLK, SIDE * HEAD), BF16),
            shape((BLK, SIDE * HEAD), BF16),
        ),
        in_specs=[vmem] * 4,
        out_specs=(vmem,) * 4,
        scratch_shapes=[
            pltpu.VMEM((SIDE, BLK, GW), BF16),
            pltpu.VMEM((SIDE, BLK, GW), BF16),
            pltpu.VMEM((SIDE, BLK, 2 * HEAD), BF16),
            pltpu.VMEM((SIDE, SIDE, BLK, 2 * HEAD), BF16),
            pltpu.VMEM((SIDE, SIDE, BLK, 2 * HEAD), BF16),
            pltpu.VMEM((3, SIDE, BLK, 2 * HEAD), BF16),
            pltpu.VMEM((3, BLK, 2 * HEAD), BF16),
            pltpu.VMEM((3, BLK, GW), BF16),
            pltpu.VMEM((3, BLK, GW), BF16),
            pltpu.VMEM((3, BLK, 2 * HEAD), BF16),
            dma((3, 2 + 2 * PARTS)),
            dma((3, 2 + 2 * PARTS)),
            dma((3, 1 + 2 * PARTS)),
            dma((3, 1 + 2 * PARTS)),
            dma((3,)),
            dma((3,)),
            dma((4,)),
            dma((4,)),
        ],
        compiler_params=pltpu.CompilerParams(
            collective_id=1, has_side_effects=True, vmem_limit_bytes=40 << 20
        ),
        name="return_rows",
    )(att, dq, dkv.reshape(SIDE, SIDE, 2, BLK, 2 * HEAD), planes)
    return o_att[None], o_dq[None], o_k[None], o_v[None]


def solution(mesh):
    rows = P("dp", "ctx", None)
    return jax.shard_map(
        body,
        mesh=mesh,
        in_specs=(rows, rows, rows, rows, P("dp", "ctx"), P("dp", "ctx")),
        out_specs=(rows,) * 4,
        check_vma=False,
    )
```

```python
import math

import jax
import jax.numpy as jnp
from jax import lax
from jax.experimental import pallas as pl
from jax.experimental.pallas import tpu as pltpu
from jax.sharding import PartitionSpec as P

MESH = pl.DeviceIdType.MESH
BF16 = jnp.bfloat16
F32 = jnp.float32

BLK = 128
HEAD = 128
GROUP = 4
GW = GROUP * HEAD
SIDE = 4
RING = 8
NBLK = 32
DOCS = 16
OFFSETS = (1, 3, 2)
CHUNK = 512
MOST = 5
PARTS = 2
PART = BLK // PARTS
FLIGHT = 2
NEG = -1e30


def place():
    x = lax.axis_index("dp")
    c = lax.axis_index("ctx")
    return x, lax.div(c, 8), lax.rem(lax.div(c, 2), 4), lax.rem(c, 2)


def remote(src, dst, send, recv, device):
    return pltpu.make_async_remote_copy(
        src_ref=src, dst_ref=dst, send_sem=send, recv_sem=recv, device_id=device, device_id_type=MESH
    )


def ahead(i, o):
    return lax.rem(i + o, 4)


def behind(i, o):
    return lax.rem(i + 4 - o, 4)


def ctx_of(z, y, core):
    return z * 8 + y * 2 + core


def lanes(i, width):
    return pl.ds(pl.multiple_of(i * width, width), width)


def one_hot(values, wanted):
    return jnp.where(values == wanted, 1.0, 0.0).astype(BF16)


def pick(weights, parts):
    width = parts[0].shape[1]
    tiles = []
    for t in range(width // 128):
        total = None
        for w, part in zip(weights, parts):
            term = part[:, t * 128 : (t + 1) * 128] * w
            total = term if total is None else total + term
        tiles.append(total)
    return tiles


def put(ref, tiles, base=None):
    for t, tile in enumerate(tiles):
        if base is None:
            ref[:, t * 128 : (t + 1) * 128] = tile
        else:
            ref[:, pl.ds(pl.multiple_of(base + t * 128, 128), 128)] = tile


def enter(devices):
    barrier = pltpu.get_barrier_semaphore()
    for device in devices:
        pl.semaphore_signal(barrier, inc=1, device_id=device, device_id_type=MESH)
    pl.semaphore_wait(barrier, len(devices))


def gather_kernel(
    q, k, v, g, seg, plan,
    qb, gb, kv, segs, planes,
    meta, a_kv, a_q, a_g, s_kv, s_q, s_g,
    xs, xr, zs, zr, ys, yr, cs, cr, fs, fr, ms, mr, os,
):
    x, z, y, core = place()
    ring = y * 2 + core
    x_dev = [(ahead(x, o), ctx_of(z, y, core)) for o in OFFSETS]
    z_dev = [(x, ctx_of(ahead(z, o), y, core)) for o in OFFSETS]
    y_dev = [(x, ctx_of(z, ahead(y, o), core)) for o in OFFSETS]
    w_dev = [(x, ctx_of(z, ahead(y, o), 1 - core)) for o in OFFSETS]
    c_dev = (x, ctx_of(z, y, 1 - core))

    meta[...] = jnp.broadcast_to(plan[...], (8, 128))
    meta[0:1, :] = seg[...]
    enter(x_dev + z_dev + y_dev + w_dev + [c_dev])

    x_cps = []

    def start_x(item):
        row = []
        for i, o in enumerate(OFFSETS):
            t = ahead(x, o)
            if item == 0:
                src, dst = meta, planes.at[x]
            elif item == 1:
                src, dst = k.at[:, lanes(t, HEAD)], a_kv.at[x, :, pl.ds(0, HEAD)]
            elif item == 2:
                src, dst = v.at[:, lanes(t, HEAD)], a_kv.at[x, :, pl.ds(HEAD, HEAD)]
            else:
                whole, land = ((q, a_q), (g, a_g))[(item - 3) // PARTS]
                rows = pl.ds(((item - 3) % PARTS) * PART, PART)
                src, dst = whole.at[rows, lanes(t, GW)], land.at[x, rows]
            cp = remote(src, dst, xs.at[i, item], xr.at[i, item], x_dev[i])
            cp.start()
            row.append(cp)
        x_cps.append(row)

    last_item = 2 + 2 * PARTS
    for item in range(3 + FLIGHT):
        start_x(item)
    planes[x] = meta[...]
    own = [
        pltpu.make_async_copy(src, dst, os.at[n])
        for n, (src, dst) in enumerate(
            (
                (k.at[:, lanes(x, HEAD)], a_kv.at[x, :, pl.ds(0, HEAD)]),
                (v.at[:, lanes(x, HEAD)], a_kv.at[x, :, pl.ds(HEAD, HEAD)]),
                (q.at[:, lanes(x, GW)], a_q.at[x]),
                (g.at[:, lanes(x, GW)], a_g.at[x]),
            )
        )
    ]
    for cp in own:
        cp.start()

    def arrived(item):
        for cp in x_cps[item]:
            cp.wait_recv()

    arrived(0)
    m_z = []
    for i, o in enumerate(OFFSETS):
        cp = remote(planes.at[ahead(z, o)], segs.at[z, ring], zs.at[i, 0], zr.at[i, 0], z_dev[i])
        cp.start()
        m_z.append(cp)
    segs[z, ring] = planes[z]
    held = [planes[d, 1:2, :] for d in range(SIDE)]
    hots = [[one_hot(h, ahead(z, o)) for h in held] for o in OFFSETS]
    own_hot = [one_hot(h, z) for h in held]

    for cp in own:
        cp.wait()
    arrived(1)
    arrived(2)
    kv_z = []
    parts = [a_kv[d] for d in range(SIDE)]
    for i, o in enumerate(OFFSETS):
        put(s_kv.at[i], pick(hots[i], parts))
        cp = remote(s_kv.at[i], kv.at[z, ring], zs.at[i, 1], zr.at[i, 1], z_dev[i])
        cp.start()
        kv_z.append(cp)
    put(kv.at[z, ring], pick(own_hot, parts))

    y_cps, c_cps, f_cps = [], [], []

    def spread(p):
        zp = z if p == 0 else behind(z, OFFSETS[p - 1])
        row = []
        for i in range(3):
            cp = remote(kv.at[zp, ring], kv.at[zp, ring], ys.at[p, i], yr.at[p, i], y_dev[i])
            cp.start()
            row.append(cp)
        y_cps.append(row)
        cp = remote(kv.at[zp, ring], kv.at[zp, ring], cs.at[p], cr.at[p], c_dev)
        cp.start()
        c_cps.append(cp)

    def pass_on(p):
        zp = z if p == 0 else behind(z, OFFSETS[p - 1])
        for i, o in enumerate(OFFSETS):
            there = behind(y, o) * 2 + core
            y_cps[p][i].wait_recv()
            cp = remote(kv.at[zp, there], kv.at[zp, there], fs.at[p, i], fr.at[p, i], c_dev)
            cp.start()
            f_cps.append(cp)

    big_z = []

    def rows_over_z(item):
        which, part = (item - 3) // PARTS, (item - 3) % PARTS
        land, stage, out = ((a_q, s_q, qb), (a_g, s_g, gb))[which]
        rows = pl.ds(part * PART, PART)
        arrived(item)
        if item + FLIGHT <= last_item:
            start_x(item + FLIGHT)
        got = [land[d, part * PART : (part + 1) * PART] for d in range(SIDE)]
        for i, o in enumerate(OFFSETS):
            put(stage.at[i, rows], pick(hots[i], got))
            cp = remote(stage.at[i, rows], out.at[z, rows], zs.at[i, item - 1], zr.at[i, item - 1], z_dev[i])
            cp.start()
            big_z.append(cp)
        put(out.at[z, rows], pick(own_hot, got))

    spread(0)
    for p in range(3):
        kv_z[p].wait_recv()
        spread(p + 1)
    for cp in m_z:
        cp.wait_recv()
    s_cps = []
    for i, device in enumerate(y_dev + w_dev + [c_dev]):
        cp = remote(segs.at[:, ring], segs.at[:, ring], ms.at[i], mr.at[i], device)
        cp.start()
        s_cps.append(cp)
    items = list(range(3, 3 + 2 * PARTS))
    for n, item in enumerate(items):
        rows_over_z(item)
        p = n - len(items) + 4
        if p >= 0:
            pass_on(p)

    for cp in big_z + c_cps + f_cps + s_cps:
        cp.wait()
    for row in x_cps:
        for cp in row:
            cp.wait_send()
    for cp in m_z + kv_z:
        cp.wait_send()
    for row in y_cps:
        for cp in row:
            cp.wait_send()


def nt(a, b):
    return lax.dot_general(a, b, (((1,), (1,)), ((), ())), preferred_element_type=F32)


def tn(a, b):
    return lax.dot_general(a, b, (((0,), (0,)), ((), ())), preferred_element_type=F32)


def nn(a, b):
    return lax.dot_general(a, b, (((1,), (0,)), ((), ())), preferred_element_type=F32)


def attend_kernel(q, g, kv, segs, att, dq, dkv, qs, gs, scores, acc, total, firsts):
    step = pl.program_id(0)
    ring = lax.rem(lax.axis_index("ctx"), 8)
    block = step * RING + ring
    scale = 1.0 / math.sqrt(HEAD)
    log2e = scale / math.log(2.0)
    heads = [slice(h * BLK, (h + 1) * BLK) for h in range(GROUP)]

    @pl.when(step == 0)
    def _():
        total[...] = jnp.zeros_like(total)
        ids = segs[:, 0, :]
        counts = jnp.concatenate(
            [jnp.sum(jnp.where(ids < t, 1.0, 0.0), axis=0, keepdims=True) for t in range(DOCS)],
            axis=0,
        )
        starts = jnp.sum(counts, axis=1, keepdims=True)
        doc = lax.broadcasted_iota(jnp.int32, (DOCS, BLK), 0)
        for n in range(SIDE):
            mine = segs[n * RING + ring, 0:1, :]
            found = jnp.sum(jnp.where(doc == mine, starts, 0.0), axis=0, keepdims=True)
            firsts[n] = jnp.broadcast_to(found.astype(jnp.int32), (8, BLK))

    for h in range(GROUP):
        qs[heads[h], :] = q[0, :, heads[h]]
        gs[heads[h], :] = g[0, :, heads[h]]

    first = firsts[step, 0:1, :]
    here = block * BLK + lax.broadcasted_iota(jnp.int32, (1, BLK), 1)
    stop = (block + 1) * BLK
    lowest = jnp.min(first.astype(F32)).astype(jnp.int32)
    count = lax.div(stop - lowest + CHUNK - 1, CHUNK)
    acc[...] = jnp.zeros_like(acc)

    def keys_of(j):
        return pl.multiple_of(jnp.maximum(stop - (j + 1) * CHUNK, 0), BLK)

    def score_step(j, top):
        base = keys_of(j)
        s = nt(kv[pl.ds(base, CHUNK), 0:HEAD], qs[...])
        pos = base + lax.broadcasted_iota(jnp.int32, (CHUNK, BLK), 0)
        seen = (pos >= first) & (pos <= jnp.minimum(here, stop - j * CHUNK - 1))
        tops = []
        for sl in heads:
            sh = jnp.where(seen, s[:, sl], NEG)
            scores[j, :, sl] = sh
            tops.append(jnp.max(sh, axis=0, keepdims=True))
        return jnp.maximum(top, jnp.concatenate(tops, axis=1))

    top = lax.fori_loop(0, count, score_step, jnp.full((1, GW), NEG, F32))

    def out_step(j, norm):
        p = jnp.exp2((scores[j] - top) * log2e)
        scores[j] = p
        acc[...] += tn(kv[pl.ds(keys_of(j), CHUNK), HEAD : 2 * HEAD], p.astype(BF16))
        return norm + jnp.sum(p, axis=0, keepdims=True)

    norm = lax.fori_loop(0, count, out_step, jnp.zeros((1, GW), F32))
    inv = 1.0 / norm
    deltas = []
    for sl in heads:
        o = jnp.transpose(acc[:, sl] * inv[:, sl]).astype(BF16)
        att[0, :, sl] = o
        prod = gs[sl, :].astype(F32) * o.astype(F32)
        deltas.append(jnp.sum(jnp.transpose(prod), axis=0, keepdims=True))
    delta = jnp.concatenate(deltas, axis=1)
    acc[...] = jnp.zeros_like(acc)

    def grad_step(j, carry):
        rows = pl.ds(keys_of(j), CHUNK)
        w = scores[j] * inv
        dp = nt(kv[rows, HEAD : 2 * HEAD], gs[...])
        ds = (w * (dp - delta)).astype(BF16)
        acc[...] += tn(kv[rows, 0:HEAD], ds)
        total[rows, 0:HEAD] += nn(ds, qs[...])
        total[rows, HEAD : 2 * HEAD] += nn(w.astype(BF16), gs[...])
        return carry

    lax.fori_loop(0, count, grad_step, 0)
    for sl in heads:
        dq[0, :, sl] = jnp.transpose(acc[:, sl] * scale).astype(BF16)

    @pl.when(step == SIDE - 1)
    def _():
        dkv[:, 0:HEAD] = (total[:, 0:HEAD] * scale).astype(BF16)
        dkv[:, HEAD : 2 * HEAD] = total[:, HEAD : 2 * HEAD].astype(BF16)


def return_kernel(
    att, dq, dkv, planes,
    o_att, o_dq, o_k, o_v,
    r_a, r_d, r_kv, c_in, tot, y_in, fin, s_a, s_d, s_kv,
    xs, xr, zs, zr, ys, yr, cs, cr,
):
    x, z, y, core = place()
    x_dev = [(ahead(x, o), ctx_of(z, y, core)) for o in OFFSETS]
    z_dev = [(x, ctx_of(ahead(z, o), y, core)) for o in OFFSETS]
    y_dev = [(x, ctx_of(z, ahead(y, o), core)) for o in OFFSETS]
    c_dev = (x, ctx_of(z, y, 1 - core))
    enter(x_dev + z_dev + y_dev + [c_dev])

    blocks = [ahead(z, o) for o in OFFSETS] + [z]
    owners = [ahead(y, o) for o in OFFSETS] + [y]
    c_cps = []
    for n, b in enumerate(blocks):
        cp = remote(dkv.at[b, :, 1 - core], c_in.at[n], cs.at[n], cr.at[n], c_dev)
        cp.start()
        c_cps.append(cp)
    z_cps = []
    for item in range(2 * PARTS):
        src, land = ((att, r_a), (dq, r_d))[item // PARTS]
        rows = pl.ds((item % PARTS) * PART, PART)
        row = []
        for i, o in enumerate(OFFSETS):
            cp = remote(src.at[ahead(z, o), rows], land.at[z, rows], zs.at[i, item], zr.at[i, item], z_dev[i])
            cp.start()
            row.append(cp)
        z_cps.append(row)
    r_a[z] = att[z]
    r_d[z] = dq[z]
    y_cps = []
    for n, b in enumerate(blocks):
        c_cps[n].wait_recv()
        row = []
        for i, owner in enumerate(owners):
            tot[n, i] = (dkv[b, owner, core].astype(F32) + c_in[n, owner].astype(F32)).astype(BF16)
            if i < 3:
                cp = remote(tot.at[n, i], y_in.at[n, i], ys.at[n, i], yr.at[n, i], y_dev[i])
                cp.start()
                row.append(cp)
        y_cps.append(row)

    x_cps = []
    hots = [[one_hot(planes[ahead(x, o), 1:2, :], s) for s in range(SIDE)] for o in OFFSETS]
    own_hot = [one_hot(planes[x, 1:2, :], s) for s in range(SIDE)]

    def rows_over_x(item):
        which, part = item // PARTS, item % PARTS
        land, stage, out = ((r_a, s_a, o_att), (r_d, s_d, o_dq))[which]
        rows = pl.ds(part * PART, PART)
        for cp in z_cps[item]:
            cp.wait_recv()
        got = [land[s, part * PART : (part + 1) * PART] for s in range(SIDE)]
        for i in range(3):
            put(stage.at[i, rows], pick(hots[i], got))
            cp = remote(
                stage.at[i, rows], out.at[rows, lanes(x, GW)], xs.at[i, item], xr.at[i, item], x_dev[i]
            )
            cp.start()
            x_cps.append(cp)
        put(out.at[rows], pick(own_hot, got), x * GW)

    f_cps = []

    def owned(n):
        total = tot[n, 3].astype(F32)
        for i in range(3):
            y_cps[n][i].wait_recv()
            total = total + y_in[n, i].astype(F32)
        if n < 3:
            fin[n] = total.astype(BF16)
            cp = remote(fin.at[n], r_kv.at[z], zs.at[n, 2 * PARTS], zr.at[n, 2 * PARTS], z_dev[n])
            cp.start()
            f_cps.append(cp)
        else:
            r_kv[z] = total.astype(BF16)

    for item in range(2 * PARTS):
        rows_over_x(item)
        n = item - 2 * PARTS + 4
        if n >= 0:
            owned(n)
    for cp in f_cps:
        cp.wait_recv()
    got = [r_kv[s] for s in range(SIDE)]
    for i in range(3):
        put(s_kv.at[i], pick(hots[i], got))
        for n, out in enumerate((o_k, o_v)):
            item = 2 * PARTS + n
            cp = remote(
                s_kv.at[i, :, pl.ds(n * HEAD, HEAD)], out.at[:, lanes(x, HEAD)],
                xs.at[i, item], xr.at[i, item], x_dev[i],
            )
            cp.start()
            x_cps.append(cp)
    mine = pick(own_hot, got)
    o_k[:, lanes(x, HEAD)] = mine[0]
    o_v[:, lanes(x, HEAD)] = mine[1]

    for cp in x_cps:
        cp.wait()
    for cp in c_cps + f_cps:
        cp.wait_send()
    for row in z_cps + y_cps:
        for cp in row:
            cp.wait_send()


def place_kernel(*refs):
    for src, dst in zip(refs[:4], refs[4:]):
        dst[...] = src[...]


def body(queries, key_rows, value_rows, out_grad, segment_ids, block_plan):
    vmem = pl.BlockSpec(memory_space=pltpu.VMEM)
    hbm = pl.BlockSpec(memory_space=pl.ANY)
    dma = pltpu.SemaphoreType.DMA
    shape = jax.ShapeDtypeStruct
    qb, gb, kv, segs, planes = pl.pallas_call(
        gather_kernel,
        out_shape=(
            shape((SIDE, BLK, GW), BF16),
            shape((SIDE, BLK, GW), BF16),
            shape((SIDE, RING, BLK, 2 * HEAD), BF16),
            shape((SIDE, RING, 8, 128), jnp.int32),
            shape((SIDE, 8, 128), jnp.int32),
        ),
        in_specs=[hbm] * 4 + [vmem] * 2,
        out_specs=(vmem,) * 5,
        scratch_shapes=[
            pltpu.VMEM((8, 128), jnp.int32),
            pltpu.VMEM((SIDE, BLK, 2 * HEAD), BF16),
            pltpu.VMEM((SIDE, BLK, GW), BF16),
            pltpu.VMEM((SIDE, BLK, GW), BF16),
            pltpu.VMEM((3, BLK, 2 * HEAD), BF16),
            pltpu.VMEM((3, BLK, GW), BF16),
            pltpu.VMEM((3, BLK, GW), BF16),
            dma((3, 3 + 2 * PARTS)),
            dma((3, 3 + 2 * PARTS)),
            dma((3, 2 + 2 * PARTS)),
            dma((3, 2 + 2 * PARTS)),
            dma((4, 3)),
            dma((4, 3)),
            dma((4,)),
            dma((4,)),
            dma((4, 3)),
            dma((4, 3)),
            dma((7,)),
            dma((7,)),
            dma((4,)),
        ],
        compiler_params=pltpu.CompilerParams(
            collective_id=0, has_side_effects=True, vmem_limit_bytes=60 << 20
        ),
        name="gather_rows",
    )(queries[0], key_rows[0], value_rows[0], out_grad[0], segment_ids, block_plan)

    rows = pl.BlockSpec((1, BLK, GW), lambda i: (i, 0, 0))
    length = NBLK * BLK
    att, dq, dkv = pl.pallas_call(
        attend_kernel,
        grid=(SIDE,),
        out_shape=(
            shape((SIDE, BLK, GW), BF16),
            shape((SIDE, BLK, GW), BF16),
            shape((length, 2 * HEAD), BF16),
        ),
        in_specs=[
            rows,
            rows,
            pl.BlockSpec((length, 2 * HEAD), lambda i: (0, 0)),
            pl.BlockSpec((NBLK, 8, 128), lambda i: (0, 0, 0)),
        ],
        out_specs=(rows, rows, pl.BlockSpec((length, 2 * HEAD), lambda i: (0, 0))),
        scratch_shapes=[
            pltpu.VMEM((GROUP * BLK, HEAD), BF16),
            pltpu.VMEM((GROUP * BLK, HEAD), BF16),
            pltpu.VMEM((MOST, CHUNK, GW), F32),
            pltpu.VMEM((HEAD, GW), F32),
            pltpu.VMEM((length, 2 * HEAD), F32),
            pltpu.VMEM((SIDE, 8, BLK), jnp.int32),
        ],
        compiler_params=pltpu.CompilerParams(vmem_limit_bytes=60 << 20),
        name="attend",
    )(qb, gb, kv.reshape(length, 2 * HEAD), segs.reshape(NBLK, 8, 128))

    o_att, o_dq, o_k, o_v = pl.pallas_call(
        return_kernel,
        out_shape=(
            shape((BLK, SIDE * GW), BF16),
            shape((BLK, SIDE * GW), BF16),
            shape((BLK, SIDE * HEAD), BF16),
            shape((BLK, SIDE * HEAD), BF16),
        ),
        in_specs=[vmem] * 4,
        out_specs=(vmem,) * 4,
        scratch_shapes=[
            pltpu.VMEM((SIDE, BLK, GW), BF16),
            pltpu.VMEM((SIDE, BLK, GW), BF16),
            pltpu.VMEM((SIDE, BLK, 2 * HEAD), BF16),
            pltpu.VMEM((SIDE, SIDE, BLK, 2 * HEAD), BF16),
            pltpu.VMEM((SIDE, SIDE, BLK, 2 * HEAD), BF16),
            pltpu.VMEM((SIDE, 3, BLK, 2 * HEAD), BF16),
            pltpu.VMEM((3, BLK, 2 * HEAD), BF16),
            pltpu.VMEM((3, BLK, GW), BF16),
            pltpu.VMEM((3, BLK, GW), BF16),
            pltpu.VMEM((3, BLK, 2 * HEAD), BF16),
            dma((3, 2 + 2 * PARTS)),
            dma((3, 2 + 2 * PARTS)),
            dma((3, 1 + 2 * PARTS)),
            dma((3, 1 + 2 * PARTS)),
            dma((4, 3)),
            dma((4, 3)),
            dma((4,)),
            dma((4,)),
        ],
        compiler_params=pltpu.CompilerParams(
            collective_id=1, has_side_effects=True, vmem_limit_bytes=60 << 20
        ),
        name="return_rows",
    )(att, dq, dkv.reshape(SIDE, SIDE, 2, BLK, 2 * HEAD), planes)
    outs = (o_att, o_dq, o_k, o_v)
    outs = pl.pallas_call(
        place_kernel,
        out_shape=tuple(shape(o.shape, BF16) for o in outs),
        in_specs=[vmem] * 4,
        out_specs=(vmem,) * 4,
        compiler_params=pltpu.CompilerParams(vmem_limit_bytes=60 << 20),
        name="place",
    )(*outs)
    return tuple(o[None] for o in outs)


def solution(mesh):
    rows = P("dp", "ctx", None)
    return jax.shard_map(
        body,
        mesh=mesh,
        in_specs=(rows, rows, rows, rows, P("dp", "ctx"), P("dp", "ctx")),
        out_specs=(rows,) * 4,
        check_vma=False,
    )
```

```python
import functools
import math

import jax
import jax.numpy as jnp
from jax import lax
from jax.experimental import pallas as pl
from jax.experimental.pallas import tpu as pltpu
from jax.sharding import PartitionSpec as P

MESH = pl.DeviceIdType.MESH
BF16 = jnp.bfloat16
F32 = jnp.float32

BLK = 128
HEAD = 128
GROUP = 4
GW = GROUP * HEAD
SIDE = 4
RING = 8
NBLK = 32
DOCS = 16
OFFSETS = (1, 3, 2)
CHUNK = 256
MOST = 10
SIZES = (1, 2, 3, 4, 5, 6, 8, 10)
PARTS = 2
PART = BLK // PARTS
FLIGHT = 2
NEG = -1e30


def place():
    x = lax.axis_index("dp")
    c = lax.axis_index("ctx")
    return x, lax.div(c, 8), lax.rem(lax.div(c, 2), 4), lax.rem(c, 2)


def remote(src, dst, send, recv, device):
    return pltpu.make_async_remote_copy(
        src_ref=src, dst_ref=dst, send_sem=send, recv_sem=recv, device_id=device, device_id_type=MESH
    )


def ahead(i, o):
    return lax.rem(i + o, 4)


def behind(i, o):
    return lax.rem(i + 4 - o, 4)


def ctx_of(z, y, core):
    return z * 8 + y * 2 + core


def lanes(i, width):
    return pl.ds(pl.multiple_of(i * width, width), width)


def one_hot(values, wanted):
    return jnp.where(values == wanted, 1.0, 0.0).astype(BF16)


def pick(weights, parts):
    width = parts[0].shape[1]
    tiles = []
    for t in range(width // 128):
        total = None
        for w, part in zip(weights, parts):
            term = part[:, t * 128 : (t + 1) * 128] * w
            total = term if total is None else total + term
        tiles.append(total)
    return tiles


def put(ref, tiles, base=None):
    for t, tile in enumerate(tiles):
        if base is None:
            ref[:, t * 128 : (t + 1) * 128] = tile
        else:
            ref[:, pl.ds(pl.multiple_of(base + t * 128, 128), 128)] = tile


def enter(devices):
    barrier = pltpu.get_barrier_semaphore()
    for device in devices:
        pl.semaphore_signal(barrier, inc=1, device_id=device, device_id_type=MESH)
    pl.semaphore_wait(barrier, len(devices))


def gather_kernel(
    q, k, v, g, seg, plan,
    qb, gb, kv, segs, planes,
    meta, a_kv, a_q, a_g, s_kv, s_q, s_g,
    xs, xr, zs, zr, ys, yr, cs, cr, fs, fr, ms, mr, os,
):
    x, z, y, core = place()
    ring = y * 2 + core
    x_dev = [(ahead(x, o), ctx_of(z, y, core)) for o in OFFSETS]
    z_dev = [(x, ctx_of(ahead(z, o), y, core)) for o in OFFSETS]
    y_dev = [(x, ctx_of(z, ahead(y, o), core)) for o in OFFSETS]
    w_dev = [(x, ctx_of(z, ahead(y, o), 1 - core)) for o in OFFSETS]
    c_dev = (x, ctx_of(z, y, 1 - core))

    meta[...] = jnp.broadcast_to(plan[...], (8, 128))
    meta[0:1, :] = seg[...]
    enter(x_dev + z_dev + y_dev + w_dev + [c_dev])

    x_cps = []

    def start_x(item):
        row = []
        for i, o in enumerate(OFFSETS):
            t = ahead(x, o)
            if item == 0:
                src, dst = meta, planes.at[x]
            elif item == 1:
                src, dst = k.at[:, lanes(t, HEAD)], a_kv.at[x, :, pl.ds(0, HEAD)]
            elif item == 2:
                src, dst = v.at[:, lanes(t, HEAD)], a_kv.at[x, :, pl.ds(HEAD, HEAD)]
            else:
                whole, land = ((q, a_q), (g, a_g))[(item - 3) // PARTS]
                rows = pl.ds(((item - 3) % PARTS) * PART, PART)
                src, dst = whole.at[rows, lanes(t, GW)], land.at[x, rows]
            cp = remote(src, dst, xs.at[i, item], xr.at[i, item], x_dev[i])
            cp.start()
            row.append(cp)
        x_cps.append(row)

    last_item = 2 + 2 * PARTS
    for item in range(3 + FLIGHT):
        start_x(item)
    planes[x] = meta[...]
    own = [
        pltpu.make_async_copy(src, dst, os.at[n])
        for n, (src, dst) in enumerate(
            (
                (k.at[:, lanes(x, HEAD)], a_kv.at[x, :, pl.ds(0, HEAD)]),
                (v.at[:, lanes(x, HEAD)], a_kv.at[x, :, pl.ds(HEAD, HEAD)]),
                (q.at[:, lanes(x, GW)], a_q.at[x]),
                (g.at[:, lanes(x, GW)], a_g.at[x]),
            )
        )
    ]
    for cp in own:
        cp.start()

    def arrived(item):
        for cp in x_cps[item]:
            cp.wait_recv()

    arrived(0)
    m_z = []
    for i, o in enumerate(OFFSETS):
        cp = remote(planes.at[ahead(z, o)], segs.at[z, ring], zs.at[i, 0], zr.at[i, 0], z_dev[i])
        cp.start()
        m_z.append(cp)
    segs[z, ring] = planes[z]
    held = [planes[d, 1:2, :] for d in range(SIDE)]
    hots = [[one_hot(h, ahead(z, o)) for h in held] for o in OFFSETS]
    own_hot = [one_hot(h, z) for h in held]

    for cp in own:
        cp.wait()
    arrived(1)
    arrived(2)
    kv_z = []
    parts = [a_kv[d] for d in range(SIDE)]
    for i, o in enumerate(OFFSETS):
        put(s_kv.at[i], pick(hots[i], parts))
        cp = remote(s_kv.at[i], kv.at[z, ring], zs.at[i, 1], zr.at[i, 1], z_dev[i])
        cp.start()
        kv_z.append(cp)
    put(kv.at[z, ring], pick(own_hot, parts))

    y_cps, c_cps, f_cps = [], [], []

    def spread(p):
        zp = z if p == 0 else behind(z, OFFSETS[p - 1])
        row = []
        for i in range(3):
            cp = remote(kv.at[zp, ring], kv.at[zp, ring], ys.at[p, i], yr.at[p, i], y_dev[i])
            cp.start()
            row.append(cp)
        y_cps.append(row)
        cp = remote(kv.at[zp, ring], kv.at[zp, ring], cs.at[p], cr.at[p], c_dev)
        cp.start()
        c_cps.append(cp)

    def pass_on(p):
        zp = z if p == 0 else behind(z, OFFSETS[p - 1])
        for i, o in enumerate(OFFSETS):
            there = behind(y, o) * 2 + core
            y_cps[p][i].wait_recv()
            cp = remote(kv.at[zp, there], kv.at[zp, there], fs.at[p, i], fr.at[p, i], c_dev)
            cp.start()
            f_cps.append(cp)

    big_z = []

    def rows_over_z(item):
        which, part = (item - 3) // PARTS, (item - 3) % PARTS
        land, stage, out = ((a_q, s_q, qb), (a_g, s_g, gb))[which]
        rows = pl.ds(part * PART, PART)
        arrived(item)
        if item + FLIGHT <= last_item:
            start_x(item + FLIGHT)
        got = [land[d, part * PART : (part + 1) * PART] for d in range(SIDE)]
        for i, o in enumerate(OFFSETS):
            put(stage.at[i, rows], pick(hots[i], got))
            cp = remote(stage.at[i, rows], out.at[z, rows], zs.at[i, item - 1], zr.at[i, item - 1], z_dev[i])
            cp.start()
            big_z.append(cp)
        put(out.at[z, rows], pick(own_hot, got))

    spread(0)
    for p in range(3):
        kv_z[p].wait_recv()
        spread(p + 1)
    for cp in m_z:
        cp.wait_recv()
    s_cps = []
    for i, device in enumerate(y_dev + w_dev + [c_dev]):
        cp = remote(segs.at[:, ring], segs.at[:, ring], ms.at[i], mr.at[i], device)
        cp.start()
        s_cps.append(cp)
    items = list(range(3, 3 + 2 * PARTS))
    for n, item in enumerate(items):
        rows_over_z(item)
        p = n - len(items) + 4
        if p >= 0:
            pass_on(p)

    for cp in big_z + c_cps + f_cps + s_cps:
        cp.wait()
    for row in x_cps:
        for cp in row:
            cp.wait_send()
    for cp in m_z + kv_z:
        cp.wait_send()
    for row in y_cps:
        for cp in row:
            cp.wait_send()


def nt(a, b):
    return lax.dot_general(a, b, (((1,), (1,)), ((), ())), preferred_element_type=F32)


def tn(a, b):
    return lax.dot_general(a, b, (((0,), (0,)), ((), ())), preferred_element_type=F32)


def nn(a, b):
    return lax.dot_general(a, b, (((1,), (0,)), ((), ())), preferred_element_type=F32)


def attend_kernel(q, g, kv, segs, att, dq, dkv, qs, gs, scores, acc, total, firsts, halves, grads):
    step = pl.program_id(0)
    ring = lax.rem(lax.axis_index("ctx"), 8)
    block = step * RING + ring
    scale = 1.0 / math.sqrt(HEAD)
    log2e = scale / math.log(2.0)
    heads = [slice(h * BLK, (h + 1) * BLK) for h in range(GROUP)]

    @pl.when(step == 0)
    def _():
        total[...] = jnp.zeros_like(total)
        ids = segs[:, 0, :]
        counts = jnp.concatenate(
            [jnp.sum(jnp.where(ids < t, 1.0, 0.0), axis=0, keepdims=True) for t in range(DOCS)],
            axis=0,
        )
        starts = jnp.sum(counts, axis=1, keepdims=True)
        doc = lax.broadcasted_iota(jnp.int32, (DOCS, BLK), 0)
        for n in range(SIDE):
            mine = segs[n * RING + ring, 0:1, :]
            found = jnp.sum(jnp.where(doc == mine, starts, 0.0), axis=0, keepdims=True)
            firsts[n] = jnp.broadcast_to(found.astype(jnp.int32), (8, BLK))

    for h in range(GROUP):
        qs[heads[h], :] = q[0, :, heads[h]]
        gs[heads[h], :] = g[0, :, heads[h]]

    first = firsts[step, 0:1, :]
    here = block * BLK + lax.broadcasted_iota(jnp.int32, (1, BLK), 1)
    stop = (block + 1) * BLK
    lowest = jnp.min(first.astype(F32)).astype(jnp.int32)
    count = lax.div(stop - lowest + CHUNK - 1, CHUNK)
    def keys_of(j):
        return pl.multiple_of(jnp.maximum(stop - (j + 1) * CHUNK, 0), BLK)

    def steps(n):
        top = jnp.full((1, GW), NEG, F32)
        for j in range(n):
            base = keys_of(j)
            s = nt(kv[pl.ds(base, CHUNK), 0:HEAD], qs[...])
            pos = base + lax.broadcasted_iota(jnp.int32, (CHUNK, BLK), 0)
            seen = (pos >= first) & (pos <= jnp.minimum(here, stop - j * CHUNK - 1))
            tops = []
            for sl in heads:
                sh = jnp.where(seen, s[:, sl], NEG)
                scores[j, :, sl] = sh
                tops.append(jnp.max(sh, axis=0, keepdims=True))
            top = jnp.maximum(top, jnp.concatenate(tops, axis=1))

        acc[...] = jnp.zeros_like(acc)

        def add_out(j):
            acc[...] += tn(kv[pl.ds(keys_of(j), CHUNK), HEAD : 2 * HEAD], halves[j])

        norm = jnp.zeros((1, GW), F32)
        for j in range(n):
            if j > 0:
                add_out(j - 1)
            p = jnp.exp2((scores[j] - top) * log2e)
            scores[j] = p
            halves[j] = p.astype(BF16)
            norm = norm + jnp.sum(p, axis=0, keepdims=True)
        add_out(n - 1)
        inv = 1.0 / norm
        deltas = []
        for sl in heads:
            o = jnp.transpose(acc[:, sl] * inv[:, sl]).astype(BF16)
            att[0, :, sl] = o
            prod = gs[sl, :].astype(F32) * o.astype(F32)
            deltas.append(jnp.sum(jnp.transpose(prod), axis=0, keepdims=True))
        delta = jnp.concatenate(deltas, axis=1)
        acc[...] = jnp.zeros_like(acc)

        def add_grads(j):
            rows = pl.ds(keys_of(j), CHUNK)
            acc[...] += tn(kv[rows, 0:HEAD], grads[j])
            total[rows, 0:HEAD] += nn(grads[j], qs[...])
            total[rows, HEAD : 2 * HEAD] += nn(halves[j], gs[...])

        for j in range(n):
            dp = nt(kv[pl.ds(keys_of(j), CHUNK), HEAD : 2 * HEAD], gs[...])
            if j > 0:
                add_grads(j - 1)
            w = scores[j] * inv
            grads[j] = (w * (dp - delta)).astype(BF16)
            halves[j] = w.astype(BF16)
        add_grads(n - 1)
        for sl in heads:
            dq[0, :, sl] = jnp.transpose(acc[:, sl] * scale).astype(BF16)

    below = 0
    for n in SIZES:
        pl.when((count > below) & (count <= n))(functools.partial(steps, n))
        below = n

    @pl.when(step == SIDE - 1)
    def _():
        dkv[:, 0:HEAD] = (total[:, 0:HEAD] * scale).astype(BF16)
        dkv[:, HEAD : 2 * HEAD] = total[:, HEAD : 2 * HEAD].astype(BF16)


def return_kernel(
    att, dq, dkv, planes,
    o_att, o_dq, o_k, o_v,
    r_a, r_d, r_kv, c_in, tot, y_in, fin, s_a, s_d, s_kv,
    xs, xr, zs, zr, ys, yr, cs, cr,
):
    x, z, y, core = place()
    x_dev = [(ahead(x, o), ctx_of(z, y, core)) for o in OFFSETS]
    z_dev = [(x, ctx_of(ahead(z, o), y, core)) for o in OFFSETS]
    y_dev = [(x, ctx_of(z, ahead(y, o), core)) for o in OFFSETS]
    c_dev = (x, ctx_of(z, y, 1 - core))
    enter(x_dev + z_dev + y_dev + [c_dev])

    blocks = [ahead(z, o) for o in OFFSETS] + [z]
    owners = [ahead(y, o) for o in OFFSETS] + [y]
    c_cps = []
    for n, b in enumerate(blocks):
        cp = remote(dkv.at[b, :, 1 - core], c_in.at[n], cs.at[n], cr.at[n], c_dev)
        cp.start()
        c_cps.append(cp)
    z_cps = []
    for item in range(2 * PARTS):
        src, land = ((att, r_a), (dq, r_d))[item // PARTS]
        rows = pl.ds((item % PARTS) * PART, PART)
        row = []
        for i, o in enumerate(OFFSETS):
            cp = remote(src.at[ahead(z, o), rows], land.at[z, rows], zs.at[i, item], zr.at[i, item], z_dev[i])
            cp.start()
            row.append(cp)
        z_cps.append(row)
    r_a[z] = att[z]
    r_d[z] = dq[z]
    y_cps = []
    for n, b in enumerate(blocks):
        c_cps[n].wait_recv()
        row = []
        for i, owner in enumerate(owners):
            tot[n, i] = (dkv[b, owner, core].astype(F32) + c_in[n, owner].astype(F32)).astype(BF16)
            if i < 3:
                cp = remote(tot.at[n, i], y_in.at[n, i], ys.at[n, i], yr.at[n, i], y_dev[i])
                cp.start()
                row.append(cp)
        y_cps.append(row)

    x_cps = []
    hots = [[one_hot(planes[ahead(x, o), 1:2, :], s) for s in range(SIDE)] for o in OFFSETS]
    own_hot = [one_hot(planes[x, 1:2, :], s) for s in range(SIDE)]

    def rows_over_x(item):
        which, part = item // PARTS, item % PARTS
        land, stage, out = ((r_a, s_a, o_att), (r_d, s_d, o_dq))[which]
        rows = pl.ds(part * PART, PART)
        for cp in z_cps[item]:
            cp.wait_recv()
        got = [land[s, part * PART : (part + 1) * PART] for s in range(SIDE)]
        for i in range(3):
            put(stage.at[i, rows], pick(hots[i], got))
            cp = remote(
                stage.at[i, rows], out.at[rows, lanes(x, GW)], xs.at[i, item], xr.at[i, item], x_dev[i]
            )
            cp.start()
            x_cps.append(cp)
        put(out.at[rows], pick(own_hot, got), x * GW)

    f_cps = []

    def owned(n):
        total = tot[n, 3].astype(F32)
        for i in range(3):
            y_cps[n][i].wait_recv()
            total = total + y_in[n, i].astype(F32)
        if n < 3:
            fin[n] = total.astype(BF16)
            cp = remote(fin.at[n], r_kv.at[z], zs.at[n, 2 * PARTS], zr.at[n, 2 * PARTS], z_dev[n])
            cp.start()
            f_cps.append(cp)
        else:
            r_kv[z] = total.astype(BF16)

    for item in range(2 * PARTS):
        rows_over_x(item)
        n = item - 2 * PARTS + 4
        if n >= 0:
            owned(n)
    for cp in f_cps:
        cp.wait_recv()
    got = [r_kv[s] for s in range(SIDE)]
    for i in range(3):
        put(s_kv.at[i], pick(hots[i], got))
        for n, out in enumerate((o_k, o_v)):
            item = 2 * PARTS + n
            cp = remote(
                s_kv.at[i, :, pl.ds(n * HEAD, HEAD)], out.at[:, lanes(x, HEAD)],
                xs.at[i, item], xr.at[i, item], x_dev[i],
            )
            cp.start()
            x_cps.append(cp)
    mine = pick(own_hot, got)
    o_k[:, lanes(x, HEAD)] = mine[0]
    o_v[:, lanes(x, HEAD)] = mine[1]

    for cp in x_cps:
        cp.wait()
    for cp in c_cps + f_cps:
        cp.wait_send()
    for row in z_cps + y_cps:
        for cp in row:
            cp.wait_send()


def place_kernel(*refs):
    for src, dst in zip(refs[:4], refs[4:]):
        dst[...] = src[...]


def body(queries, key_rows, value_rows, out_grad, segment_ids, block_plan):
    vmem = pl.BlockSpec(memory_space=pltpu.VMEM)
    hbm = pl.BlockSpec(memory_space=pl.ANY)
    dma = pltpu.SemaphoreType.DMA
    shape = jax.ShapeDtypeStruct
    qb, gb, kv, segs, planes = pl.pallas_call(
        gather_kernel,
        out_shape=(
            shape((SIDE, BLK, GW), BF16),
            shape((SIDE, BLK, GW), BF16),
            shape((SIDE, RING, BLK, 2 * HEAD), BF16),
            shape((SIDE, RING, 8, 128), jnp.int32),
            shape((SIDE, 8, 128), jnp.int32),
        ),
        in_specs=[hbm] * 4 + [vmem] * 2,
        out_specs=(vmem,) * 5,
        scratch_shapes=[
            pltpu.VMEM((8, 128), jnp.int32),
            pltpu.VMEM((SIDE, BLK, 2 * HEAD), BF16),
            pltpu.VMEM((SIDE, BLK, GW), BF16),
            pltpu.VMEM((SIDE, BLK, GW), BF16),
            pltpu.VMEM((3, BLK, 2 * HEAD), BF16),
            pltpu.VMEM((3, BLK, GW), BF16),
            pltpu.VMEM((3, BLK, GW), BF16),
            dma((3, 3 + 2 * PARTS)),
            dma((3, 3 + 2 * PARTS)),
            dma((3, 2 + 2 * PARTS)),
            dma((3, 2 + 2 * PARTS)),
            dma((4, 3)),
            dma((4, 3)),
            dma((4,)),
            dma((4,)),
            dma((4, 3)),
            dma((4, 3)),
            dma((7,)),
            dma((7,)),
            dma((4,)),
        ],
        compiler_params=pltpu.CompilerParams(
            collective_id=0, has_side_effects=True, vmem_limit_bytes=60 << 20
        ),
        name="gather_rows",
    )(queries[0], key_rows[0], value_rows[0], out_grad[0], segment_ids, block_plan)

    rows = pl.BlockSpec((1, BLK, GW), lambda i: (i, 0, 0))
    length = NBLK * BLK
    att, dq, dkv = pl.pallas_call(
        attend_kernel,
        grid=(SIDE,),
        out_shape=(
            shape((SIDE, BLK, GW), BF16),
            shape((SIDE, BLK, GW), BF16),
            shape((length, 2 * HEAD), BF16),
        ),
        in_specs=[
            rows,
            rows,
            pl.BlockSpec((length, 2 * HEAD), lambda i: (0, 0)),
            pl.BlockSpec((NBLK, 8, 128), lambda i: (0, 0, 0)),
        ],
        out_specs=(rows, rows, pl.BlockSpec((length, 2 * HEAD), lambda i: (0, 0))),
        scratch_shapes=[
            pltpu.VMEM((GROUP * BLK, HEAD), BF16),
            pltpu.VMEM((GROUP * BLK, HEAD), BF16),
            pltpu.VMEM((MOST, CHUNK, GW), F32),
            pltpu.VMEM((HEAD, GW), F32),
            pltpu.VMEM((length, 2 * HEAD), F32),
            pltpu.VMEM((SIDE, 8, BLK), jnp.int32),
            pltpu.VMEM((MOST, CHUNK, GW), BF16),
            pltpu.VMEM((MOST, CHUNK, GW), BF16),
        ],
        compiler_params=pltpu.CompilerParams(vmem_limit_bytes=60 << 20),
        name="attend",
    )(qb, gb, kv.reshape(length, 2 * HEAD), segs.reshape(NBLK, 8, 128))

    o_att, o_dq, o_k, o_v = pl.pallas_call(
        return_kernel,
        out_shape=(
            shape((BLK, SIDE * GW), BF16),
            shape((BLK, SIDE * GW), BF16),
            shape((BLK, SIDE * HEAD), BF16),
            shape((BLK, SIDE * HEAD), BF16),
        ),
        in_specs=[vmem] * 4,
        out_specs=(vmem,) * 4,
        scratch_shapes=[
            pltpu.VMEM((SIDE, BLK, GW), BF16),
            pltpu.VMEM((SIDE, BLK, GW), BF16),
            pltpu.VMEM((SIDE, BLK, 2 * HEAD), BF16),
            pltpu.VMEM((SIDE, SIDE, BLK, 2 * HEAD), BF16),
            pltpu.VMEM((SIDE, SIDE, BLK, 2 * HEAD), BF16),
            pltpu.VMEM((SIDE, 3, BLK, 2 * HEAD), BF16),
            pltpu.VMEM((3, BLK, 2 * HEAD), BF16),
            pltpu.VMEM((3, BLK, GW), BF16),
            pltpu.VMEM((3, BLK, GW), BF16),
            pltpu.VMEM((3, BLK, 2 * HEAD), BF16),
            dma((3, 2 + 2 * PARTS)),
            dma((3, 2 + 2 * PARTS)),
            dma((3, 1 + 2 * PARTS)),
            dma((3, 1 + 2 * PARTS)),
            dma((4, 3)),
            dma((4, 3)),
            dma((4,)),
            dma((4,)),
        ],
        compiler_params=pltpu.CompilerParams(
            collective_id=1, has_side_effects=True, vmem_limit_bytes=60 << 20
        ),
        name="return_rows",
    )(att, dq, dkv.reshape(SIDE, SIDE, 2, BLK, 2 * HEAD), planes)
    outs = (o_att, o_dq, o_k, o_v)
    outs = pl.pallas_call(
        place_kernel,
        out_shape=tuple(shape(o.shape, BF16) for o in outs),
        in_specs=[vmem] * 4,
        out_specs=(vmem,) * 4,
        compiler_params=pltpu.CompilerParams(vmem_limit_bytes=60 << 20),
        name="place",
    )(*outs)
    return tuple(o[None] for o in outs)


def solution(mesh):
    rows = P("dp", "ctx", None)
    return jax.shard_map(
        body,
        mesh=mesh,
        in_specs=(rows, rows, rows, rows, P("dp", "ctx"), P("dp", "ctx")),
        out_specs=(rows,) * 4,
        check_vma=False,
    )
```

```python
import functools
import math

import jax
import jax.numpy as jnp
from jax import lax
from jax.experimental import pallas as pl
from jax.experimental.pallas import tpu as pltpu
from jax.sharding import PartitionSpec as P

MESH = pl.DeviceIdType.MESH
BF16 = jnp.bfloat16
F32 = jnp.float32

BLK = 128
HEAD = 128
GROUP = 4
GW = GROUP * HEAD
SIDE = 4
RING = 8
NBLK = 32
DOCS = 16
OFFSETS = (1, 3, 2)
CHUNK = 256
MOST = 10
SIZES = (1, 2, 3, 4, 5, 6, 8, 10)
PARTS = 2
PART = BLK // PARTS
FLIGHT = 2
NEG = -1e30


def place():
    x = lax.axis_index("dp")
    c = lax.axis_index("ctx")
    return x, lax.div(c, 8), lax.rem(lax.div(c, 2), 4), lax.rem(c, 2)


def remote(src, dst, send, recv, device):
    return pltpu.make_async_remote_copy(
        src_ref=src, dst_ref=dst, send_sem=send, recv_sem=recv, device_id=device, device_id_type=MESH
    )


def ahead(i, o):
    return lax.rem(i + o, 4)


def behind(i, o):
    return lax.rem(i + 4 - o, 4)


def ctx_of(z, y, core):
    return z * 8 + y * 2 + core


def lanes(i, width):
    return pl.ds(pl.multiple_of(i * width, width), width)


def one_hot(values, wanted):
    return jnp.where(values == wanted, 1.0, 0.0).astype(BF16)


def pick(weights, parts):
    width = parts[0].shape[1]
    tiles = []
    for t in range(width // 128):
        total = None
        for w, part in zip(weights, parts):
            term = part[:, t * 128 : (t + 1) * 128] * w
            total = term if total is None else total + term
        tiles.append(total)
    return tiles


def put(ref, tiles, base=None):
    for t, tile in enumerate(tiles):
        if base is None:
            ref[:, t * 128 : (t + 1) * 128] = tile
        else:
            ref[:, pl.ds(pl.multiple_of(base + t * 128, 128), 128)] = tile


def enter(devices):
    barrier = pltpu.get_barrier_semaphore()
    for device in devices:
        pl.semaphore_signal(barrier, inc=1, device_id=device, device_id_type=MESH)
    pl.semaphore_wait(barrier, len(devices))


def gather_kernel(
    q, k, v, g, seg, plan,
    qb, gb, kv, segs, planes,
    meta, a_kv, a_q, a_g, s_kv, s_q, s_g,
    xs, xr, zs, zr, ys, yr, cs, cr, fs, fr, ms, mr, os,
):
    x, z, y, core = place()
    ring = y * 2 + core
    x_dev = [(ahead(x, o), ctx_of(z, y, core)) for o in OFFSETS]
    z_dev = [(x, ctx_of(ahead(z, o), y, core)) for o in OFFSETS]
    y_dev = [(x, ctx_of(z, ahead(y, o), core)) for o in OFFSETS]
    w_dev = [(x, ctx_of(z, ahead(y, o), 1 - core)) for o in OFFSETS]
    c_dev = (x, ctx_of(z, y, 1 - core))

    meta[...] = jnp.broadcast_to(plan[...], (8, 128))
    meta[0:1, :] = seg[...]
    enter(x_dev + z_dev + y_dev + w_dev + [c_dev])

    x_cps = []

    def start_x(item):
        row = []
        for i, o in enumerate(OFFSETS):
            t = ahead(x, o)
            if item == 0:
                src, dst = meta, planes.at[x]
            elif item == 1:
                src, dst = k.at[:, lanes(t, HEAD)], a_kv.at[x, :, pl.ds(0, HEAD)]
            elif item == 2:
                src, dst = v.at[:, lanes(t, HEAD)], a_kv.at[x, :, pl.ds(HEAD, HEAD)]
            else:
                whole, land = ((q, a_q), (g, a_g))[(item - 3) // PARTS]
                rows = pl.ds(((item - 3) % PARTS) * PART, PART)
                src, dst = whole.at[rows, lanes(t, GW)], land.at[x, rows]
            cp = remote(src, dst, xs.at[i, item], xr.at[i, item], x_dev[i])
            cp.start()
            row.append(cp)
        x_cps.append(row)

    last_item = 2 + 2 * PARTS
    for item in range(3 + FLIGHT):
        start_x(item)
    planes[x] = meta[...]
    own = [
        pltpu.make_async_copy(src, dst, os.at[n])
        for n, (src, dst) in enumerate(
            (
                (k.at[:, lanes(x, HEAD)], a_kv.at[x, :, pl.ds(0, HEAD)]),
                (v.at[:, lanes(x, HEAD)], a_kv.at[x, :, pl.ds(HEAD, HEAD)]),
                (q.at[:, lanes(x, GW)], a_q.at[x]),
                (g.at[:, lanes(x, GW)], a_g.at[x]),
            )
        )
    ]
    for cp in own:
        cp.start()

    def arrived(item):
        for cp in x_cps[item]:
            cp.wait_recv()

    arrived(0)
    m_z = []
    for i, o in enumerate(OFFSETS):
        cp = remote(planes.at[ahead(z, o)], segs.at[z, ring], zs.at[i, 0], zr.at[i, 0], z_dev[i])
        cp.start()
        m_z.append(cp)
    segs[z, ring] = planes[z]
    held = [planes[d, 1:2, :] for d in range(SIDE)]
    hots = [[one_hot(h, ahead(z, o)) for h in held] for o in OFFSETS]
    own_hot = [one_hot(h, z) for h in held]

    for cp in own:
        cp.wait()
    arrived(1)
    arrived(2)
    kv_z = []
    parts = [a_kv[d] for d in range(SIDE)]
    for i, o in enumerate(OFFSETS):
        put(s_kv.at[i], pick(hots[i], parts))
        cp = remote(s_kv.at[i], kv.at[z, ring], zs.at[i, 1], zr.at[i, 1], z_dev[i])
        cp.start()
        kv_z.append(cp)
    put(kv.at[z, ring], pick(own_hot, parts))

    y_cps, c_cps, f_cps = [], [], []

    def spread(p):
        zp = z if p == 0 else behind(z, OFFSETS[p - 1])
        row = []
        for i in range(3):
            cp = remote(kv.at[zp, ring], kv.at[zp, ring], ys.at[p, i], yr.at[p, i], y_dev[i])
            cp.start()
            row.append(cp)
        y_cps.append(row)
        cp = remote(kv.at[zp, ring], kv.at[zp, ring], cs.at[p], cr.at[p], c_dev)
        cp.start()
        c_cps.append(cp)

    def pass_on(p):
        zp = z if p == 0 else behind(z, OFFSETS[p - 1])
        for i, o in enumerate(OFFSETS):
            there = behind(y, o) * 2 + core
            y_cps[p][i].wait_recv()
            cp = remote(kv.at[zp, there], kv.at[zp, there], fs.at[p, i], fr.at[p, i], c_dev)
            cp.start()
            f_cps.append(cp)

    big_z = []

    def rows_over_z(item):
        which, part = (item - 3) // PARTS, (item - 3) % PARTS
        land, stage, out = ((a_q, s_q, qb), (a_g, s_g, gb))[which]
        rows = pl.ds(part * PART, PART)
        arrived(item)
        if item + FLIGHT <= last_item:
            start_x(item + FLIGHT)
        got = [land[d, part * PART : (part + 1) * PART] for d in range(SIDE)]
        for i, o in enumerate(OFFSETS):
            put(stage.at[i, rows], pick(hots[i], got))
            cp = remote(stage.at[i, rows], out.at[z, rows], zs.at[i, item - 1], zr.at[i, item - 1], z_dev[i])
            cp.start()
            big_z.append(cp)
        put(out.at[z, rows], pick(own_hot, got))

    spread(0)
    for p in range(3):
        kv_z[p].wait_recv()
        spread(p + 1)
    for cp in m_z:
        cp.wait_recv()
    s_cps = []
    for i, device in enumerate(y_dev + w_dev + [c_dev]):
        cp = remote(segs.at[:, ring], segs.at[:, ring], ms.at[i], mr.at[i], device)
        cp.start()
        s_cps.append(cp)
    items = list(range(3, 3 + 2 * PARTS))
    for n, item in enumerate(items):
        rows_over_z(item)
        p = n - len(items) + 4
        if p >= 0:
            pass_on(p)

    for cp in big_z + c_cps + f_cps + s_cps:
        cp.wait()
    for row in x_cps:
        for cp in row:
            cp.wait_send()
    for cp in m_z + kv_z:
        cp.wait_send()
    for row in y_cps:
        for cp in row:
            cp.wait_send()


def nt(a, b):
    return lax.dot_general(a, b, (((1,), (1,)), ((), ())), preferred_element_type=F32)


def tn(a, b):
    return lax.dot_general(a, b, (((0,), (0,)), ((), ())), preferred_element_type=F32)


def nn(a, b):
    return lax.dot_general(a, b, (((1,), (0,)), ((), ())), preferred_element_type=F32)


def attend_kernel(q, g, kv, segs, att, dq, dkv, qs, gs, scores, acc, total, firsts, halves, grads):
    step = pl.program_id(0)
    ring = lax.rem(lax.axis_index("ctx"), 8)
    block = step * RING + ring
    scale = 1.0 / math.sqrt(HEAD)
    log2e = scale / math.log(2.0)
    heads = [slice(h * BLK, (h + 1) * BLK) for h in range(GROUP)]

    @pl.when(step == 0)
    def _():
        total[...] = jnp.zeros_like(total)
        ids = segs[:, 0, :]
        counts = jnp.concatenate(
            [jnp.sum(jnp.where(ids < t, 1.0, 0.0), axis=0, keepdims=True) for t in range(DOCS)],
            axis=0,
        )
        starts = jnp.sum(counts, axis=1, keepdims=True)
        doc = lax.broadcasted_iota(jnp.int32, (DOCS, BLK), 0)
        for n in range(SIDE):
            mine = segs[n * RING + ring, 0:1, :]
            found = jnp.sum(jnp.where(doc == mine, starts, 0.0), axis=0, keepdims=True)
            firsts[n] = jnp.broadcast_to(found.astype(jnp.int32), (8, BLK))

    for h in range(GROUP):
        qs[heads[h], :] = q[0, :, heads[h]]
        gs[heads[h], :] = g[0, :, heads[h]]

    first = firsts[step, 0:1, :]
    here = block * BLK + lax.broadcasted_iota(jnp.int32, (1, BLK), 1)
    stop = (block + 1) * BLK
    lowest = jnp.min(first.astype(F32)).astype(jnp.int32)
    count = lax.div(stop - lowest + CHUNK - 1, CHUNK)
    def keys_of(j):
        return pl.multiple_of(jnp.maximum(stop - (j + 1) * CHUNK, 0), BLK)

    def steps(n):
        top = jnp.full((1, GW), NEG, F32)
        for j in range(n):
            base = keys_of(j)
            s = nt(kv[pl.ds(base, CHUNK), 0:HEAD], qs[...])
            pos = base + lax.broadcasted_iota(jnp.int32, (CHUNK, BLK), 0)
            seen = (pos >= first) & (pos <= jnp.minimum(here, stop - j * CHUNK - 1))
            tops = []
            for sl in heads:
                sh = jnp.where(seen, s[:, sl], NEG)
                scores[j, :, sl] = sh
                tops.append(jnp.max(sh, axis=0, keepdims=True))
            top = jnp.maximum(top, jnp.concatenate(tops, axis=1))

        acc[...] = jnp.zeros_like(acc)

        def add_out(j):
            acc[...] += tn(kv[pl.ds(keys_of(j), CHUNK), HEAD : 2 * HEAD], halves[j])

        norm = jnp.zeros((1, GW), F32)
        for j in range(n):
            if j > 0:
                add_out(j - 1)
            p = jnp.exp2((scores[j] - top) * log2e)
            scores[j] = p
            halves[j] = p.astype(BF16)
            norm = norm + jnp.sum(p, axis=0, keepdims=True)
        add_out(n - 1)
        inv = 1.0 / norm
        deltas = []
        for sl in heads:
            o = jnp.transpose(acc[:, sl] * inv[:, sl]).astype(BF16)
            att[0, :, sl] = o
            prod = gs[sl, :].astype(F32) * o.astype(F32)
            deltas.append(jnp.sum(jnp.transpose(prod), axis=0, keepdims=True))
        delta = jnp.concatenate(deltas, axis=1)
        acc[...] = jnp.zeros_like(acc)

        def add_grads(j):
            rows = pl.ds(keys_of(j), CHUNK)
            acc[...] += tn(kv[rows, 0:HEAD], grads[j])
            total[rows, 0:HEAD] += nn(grads[j], qs[...])
            total[rows, HEAD : 2 * HEAD] += nn(halves[j], gs[...])

        for j in range(n):
            dp = nt(kv[pl.ds(keys_of(j), CHUNK), HEAD : 2 * HEAD], gs[...])
            if j > 0:
                add_grads(j - 1)
            w = scores[j] * inv
            grads[j] = (w * (dp - delta)).astype(BF16)
            halves[j] = w.astype(BF16)
        add_grads(n - 1)
        for sl in heads:
            dq[0, :, sl] = jnp.transpose(acc[:, sl] * scale).astype(BF16)

    below = 0
    for n in SIZES:
        pl.when((count > below) & (count <= n))(functools.partial(steps, n))
        below = n

    @pl.when(step == SIDE - 1)
    def _():
        dkv[:, 0:HEAD] = (total[:, 0:HEAD] * scale).astype(BF16)
        dkv[:, HEAD : 2 * HEAD] = total[:, HEAD : 2 * HEAD].astype(BF16)


def return_kernel(
    att, dq, dkv, planes,
    o_att, o_dq, o_k, o_v,
    r_a, r_d, r_kv, c_in, tot, y_in, fin, s_a, s_d, s_kv,
    xs, xr, zs, zr, ys, yr, cs, cr,
):
    x, z, y, core = place()
    x_dev = [(ahead(x, o), ctx_of(z, y, core)) for o in OFFSETS]
    z_dev = [(x, ctx_of(ahead(z, o), y, core)) for o in OFFSETS]
    y_dev = [(x, ctx_of(z, ahead(y, o), core)) for o in OFFSETS]
    c_dev = (x, ctx_of(z, y, 1 - core))
    enter(x_dev + z_dev + y_dev + [c_dev])

    blocks = [ahead(z, o) for o in OFFSETS] + [z]
    owners = [ahead(y, o) for o in OFFSETS] + [y]
    c_cps = []
    for n, b in enumerate(blocks):
        cp = remote(dkv.at[b, :, 1 - core], c_in.at[n], cs.at[n], cr.at[n], c_dev)
        cp.start()
        c_cps.append(cp)
    z_cps = []
    for item in range(2 * PARTS):
        src, land = ((att, r_a), (dq, r_d))[item // PARTS]
        rows = pl.ds((item % PARTS) * PART, PART)
        row = []
        for i, o in enumerate(OFFSETS):
            cp = remote(src.at[ahead(z, o), rows], land.at[z, rows], zs.at[i, item], zr.at[i, item], z_dev[i])
            cp.start()
            row.append(cp)
        z_cps.append(row)
    r_a[z] = att[z]
    r_d[z] = dq[z]
    y_cps = []
    for n, b in enumerate(blocks):
        c_cps[n].wait_recv()
        row = []
        for i, owner in enumerate(owners):
            tot[n, i] = (dkv[b, owner, core].astype(F32) + c_in[n, owner].astype(F32)).astype(BF16)
            if i < 3:
                cp = remote(tot.at[n, i], y_in.at[n, i], ys.at[n, i], yr.at[n, i], y_dev[i])
                cp.start()
                row.append(cp)
        y_cps.append(row)

    x_cps = []
    hots = [[one_hot(planes[ahead(x, o), 1:2, :], s) for s in range(SIDE)] for o in OFFSETS]
    own_hot = [one_hot(planes[x, 1:2, :], s) for s in range(SIDE)]

    def rows_over_x(item):
        which, part = item // PARTS, item % PARTS
        land, stage, out = ((r_a, s_a, o_att), (r_d, s_d, o_dq))[which]
        rows = pl.ds(part * PART, PART)
        for cp in z_cps[item]:
            cp.wait_recv()
        got = [land[s, part * PART : (part + 1) * PART] for s in range(SIDE)]
        for i in range(3):
            put(stage.at[i, rows], pick(hots[i], got))
            cp = remote(
                stage.at[i, rows], out.at[rows, lanes(x, GW)], xs.at[i, item], xr.at[i, item], x_dev[i]
            )
            cp.start()
            x_cps.append(cp)
        put(out.at[rows], pick(own_hot, got), x * GW)

    f_cps = []

    def owned(n):
        total = tot[n, 3].astype(F32)
        for i in range(3):
            y_cps[n][i].wait_recv()
            total = total + y_in[n, i].astype(F32)
        if n < 3:
            fin[n] = total.astype(BF16)
            cp = remote(fin.at[n], r_kv.at[z], zs.at[n, 2 * PARTS], zr.at[n, 2 * PARTS], z_dev[n])
            cp.start()
            f_cps.append(cp)
        else:
            r_kv[z] = total.astype(BF16)

    for item in range(2 * PARTS):
        rows_over_x(item)
        n = item - 2 * PARTS + 4
        if n >= 0:
            owned(n)
    for cp in f_cps:
        cp.wait_recv()
    got = [r_kv[s] for s in range(SIDE)]
    for i in range(3):
        put(s_kv.at[i], pick(hots[i], got))
        for n, out in enumerate((o_k, o_v)):
            item = 2 * PARTS + n
            cp = remote(
                s_kv.at[i, :, pl.ds(n * HEAD, HEAD)], out.at[:, lanes(x, HEAD)],
                xs.at[i, item], xr.at[i, item], x_dev[i],
            )
            cp.start()
            x_cps.append(cp)
    mine = pick(own_hot, got)
    o_k[:, lanes(x, HEAD)] = mine[0]
    o_v[:, lanes(x, HEAD)] = mine[1]

    for cp in x_cps:
        cp.wait()
    for cp in c_cps + f_cps:
        cp.wait_send()
    for row in z_cps + y_cps:
        for cp in row:
            cp.wait_send()


def place_kernel(*refs):
    srcs, dsts, held, sems = refs[:4], refs[4:8], refs[8:12], refs[12]
    ins = [pltpu.make_async_copy(srcs[n], held[n], sems.at[0, n]) for n in range(4)]
    outs = [pltpu.make_async_copy(held[n], dsts[n], sems.at[1, n]) for n in range(4)]
    for cp in ins:
        cp.start()
    for n in range(4):
        ins[n].wait()
        outs[n].start()
    for cp in outs:
        cp.wait()


def body(queries, key_rows, value_rows, out_grad, segment_ids, block_plan):
    vmem = pl.BlockSpec(memory_space=pltpu.VMEM)
    hbm = pl.BlockSpec(memory_space=pl.ANY)
    dma = pltpu.SemaphoreType.DMA
    shape = jax.ShapeDtypeStruct
    qb, gb, kv, segs, planes = pl.pallas_call(
        gather_kernel,
        out_shape=(
            shape((SIDE, BLK, GW), BF16),
            shape((SIDE, BLK, GW), BF16),
            shape((SIDE, RING, BLK, 2 * HEAD), BF16),
            shape((SIDE, RING, 8, 128), jnp.int32),
            shape((SIDE, 8, 128), jnp.int32),
        ),
        in_specs=[hbm] * 4 + [vmem] * 2,
        out_specs=(vmem,) * 5,
        scratch_shapes=[
            pltpu.VMEM((8, 128), jnp.int32),
            pltpu.VMEM((SIDE, BLK, 2 * HEAD), BF16),
            pltpu.VMEM((SIDE, BLK, GW), BF16),
            pltpu.VMEM((SIDE, BLK, GW), BF16),
            pltpu.VMEM((3, BLK, 2 * HEAD), BF16),
            pltpu.VMEM((3, BLK, GW), BF16),
            pltpu.VMEM((3, BLK, GW), BF16),
            dma((3, 3 + 2 * PARTS)),
            dma((3, 3 + 2 * PARTS)),
            dma((3, 2 + 2 * PARTS)),
            dma((3, 2 + 2 * PARTS)),
            dma((4, 3)),
            dma((4, 3)),
            dma((4,)),
            dma((4,)),
            dma((4, 3)),
            dma((4, 3)),
            dma((7,)),
            dma((7,)),
            dma((4,)),
        ],
        compiler_params=pltpu.CompilerParams(
            collective_id=0, has_side_effects=True, vmem_limit_bytes=60 << 20
        ),
        name="gather_rows",
    )(queries[0], key_rows[0], value_rows[0], out_grad[0], segment_ids, block_plan)

    rows = pl.BlockSpec((1, BLK, GW), lambda i: (i, 0, 0))
    length = NBLK * BLK
    att, dq, dkv = pl.pallas_call(
        attend_kernel,
        grid=(SIDE,),
        out_shape=(
            shape((SIDE, BLK, GW), BF16),
            shape((SIDE, BLK, GW), BF16),
            shape((length, 2 * HEAD), BF16),
        ),
        in_specs=[
            rows,
            rows,
            pl.BlockSpec((length, 2 * HEAD), lambda i: (0, 0)),
            pl.BlockSpec((NBLK, 8, 128), lambda i: (0, 0, 0)),
        ],
        out_specs=(rows, rows, pl.BlockSpec((length, 2 * HEAD), lambda i: (0, 0))),
        scratch_shapes=[
            pltpu.VMEM((GROUP * BLK, HEAD), BF16),
            pltpu.VMEM((GROUP * BLK, HEAD), BF16),
            pltpu.VMEM((MOST, CHUNK, GW), F32),
            pltpu.VMEM((HEAD, GW), F32),
            pltpu.VMEM((length, 2 * HEAD), F32),
            pltpu.VMEM((SIDE, 8, BLK), jnp.int32),
            pltpu.VMEM((MOST, CHUNK, GW), BF16),
            pltpu.VMEM((MOST, CHUNK, GW), BF16),
        ],
        compiler_params=pltpu.CompilerParams(vmem_limit_bytes=60 << 20),
        name="attend",
    )(qb, gb, kv.reshape(length, 2 * HEAD), segs.reshape(NBLK, 8, 128))

    o_att, o_dq, o_k, o_v = pl.pallas_call(
        return_kernel,
        out_shape=(
            shape((BLK, SIDE * GW), BF16),
            shape((BLK, SIDE * GW), BF16),
            shape((BLK, SIDE * HEAD), BF16),
            shape((BLK, SIDE * HEAD), BF16),
        ),
        in_specs=[vmem] * 4,
        out_specs=(vmem,) * 4,
        scratch_shapes=[
            pltpu.VMEM((SIDE, BLK, GW), BF16),
            pltpu.VMEM((SIDE, BLK, GW), BF16),
            pltpu.VMEM((SIDE, BLK, 2 * HEAD), BF16),
            pltpu.VMEM((SIDE, SIDE, BLK, 2 * HEAD), BF16),
            pltpu.VMEM((SIDE, SIDE, BLK, 2 * HEAD), BF16),
            pltpu.VMEM((SIDE, 3, BLK, 2 * HEAD), BF16),
            pltpu.VMEM((3, BLK, 2 * HEAD), BF16),
            pltpu.VMEM((3, BLK, GW), BF16),
            pltpu.VMEM((3, BLK, GW), BF16),
            pltpu.VMEM((3, BLK, 2 * HEAD), BF16),
            dma((3, 2 + 2 * PARTS)),
            dma((3, 2 + 2 * PARTS)),
            dma((3, 1 + 2 * PARTS)),
            dma((3, 1 + 2 * PARTS)),
            dma((4, 3)),
            dma((4, 3)),
            dma((4,)),
            dma((4,)),
        ],
        compiler_params=pltpu.CompilerParams(
            collective_id=1, has_side_effects=True, vmem_limit_bytes=60 << 20
        ),
        name="return_rows",
    )(att, dq, dkv.reshape(SIDE, SIDE, 2, BLK, 2 * HEAD), planes)
    outs = (o_att, o_dq, o_k, o_v)
    outs = pl.pallas_call(
        place_kernel,
        out_shape=tuple(shape(o.shape, BF16) for o in outs),
        in_specs=[hbm] * 4,
        out_specs=(hbm,) * 4,
        scratch_shapes=[pltpu.VMEM(o.shape, BF16) for o in outs] + [dma((2, 4))],
        compiler_params=pltpu.CompilerParams(vmem_limit_bytes=60 << 20),
        name="place",
    )(*outs)
    return tuple(o[None] for o in outs)


def solution(mesh):
    rows = P("dp", "ctx", None)
    return jax.shard_map(
        body,
        mesh=mesh,
        in_specs=(rows, rows, rows, rows, P("dp", "ctx"), P("dp", "ctx")),
        out_specs=(rows,) * 4,
        check_vma=False,
    )
```
